32 devices in a mesh: view: 2 (over x), seq: 4 (over y, core), event: 4 (over z).
Axes of the slice: x: 2, y: 2, z: 4, core: 2. Of those that a mesh axis runs over, the one named last changes fastest.
Arguments:
- query: bfloat16 [4, 2, 1536, 512], P('event', 'view', 'seq'), may hold values from -7 to 7
- key: bfloat16 [4, 2, 1536, 512], P('event', 'view', 'seq'), may hold values from -7 to 7
- value: bfloat16 [4, 2, 1536, 512], P('event', 'view', 'seq'), may hold values from -6 to 6
- pattern: int32 [4, 2, 12, 12], P('event', 'view', 'seq'), may hold values from 0 to 1, as said below
- out_weight: bfloat16 [512, 512], replicated, may hold values from -0.25 to 0.25
- served: int32 [4, 2, 32, 128], P('event', 'view', 'seq'), may hold values from 0 to 383
- anchor_rows: int32 [4, 2, 1024], P('event', 'view', 'seq'), may hold values from 0 to 383
- positive_slot: int32 [4, 2, 1024], P('event', 'view', 'seq'), may hold values from 0 to 1023, as said below
- anchor_live: int32 [4, 2, 1024], P('event', 'view', 'seq'), may hold values from 0 to 1, as said below
Outputs:
- mixed: bfloat16 [4, 2, 1536, 512], P('event', 'view', 'seq')
- grad_wo: float32 [512, 512], replicated
- loss: float32 [], replicated
The draws below stay inside these ranges and needn't reach their ends.
Inputs may be any that keep to these rules, and one draw needn't show every extreme that they name: pattern[e, v, b, b] is 1 for every block b. `positive_slot`: for an anchor of view v the slot lies in [(1 - v) * 512, (2 - v) * 512), a point of the other view. `anchor_live`: every device's block of 256 anchors holds at least one live anchor.
All inputs are finite; a program needn't handle non-finite values.
Results may differ from the reference program's by a relative error of at most 0.015.
Values may be sent and summed in bfloat16 or wider, within the bound.
A program may use at most 64 MiB of HBM per device.

```python
import jax
import jax.numpy as jnp
from jax import lax

D = 512
HEADS = 16
BLOCK = 128
PTS_DEV = 384
CAP = 128
PAIRS_DEV = 256
EVENTS = 4
NPTS = 1536
NB = 12
REQS = 32
CANDS = 1024
PAIRS = 1024
N_SEQ = 4


def draw_query(key, part):
    shape = (EVENTS, 2, NPTS, D)
    base = jnp.clip(1.5 * jax.random.normal(jax.random.fold_in(key, 1), shape, jnp.float32), -7.0, 7.0)
    return base.astype(jnp.bfloat16)


def draw_key(key, part):
    shape = (EVENTS, 2, NPTS, D)
    base = jnp.clip(1.5 * jax.random.normal(jax.random.fold_in(key, 2), shape, jnp.float32), -7.0, 7.0)
    return base.astype(jnp.bfloat16)


def draw_pattern(key, part):
    level = jax.random.randint(jax.random.fold_in(key, 7), (EVENTS, 2, NB, 1), 1, 9)
    rolled = jax.random.randint(jax.random.fold_in(key, 8), (EVENTS, 2, NB, NB), 0, 16)
    diagonal = jnp.arange(NB)[:, None] == jnp.arange(NB)[None, :]
    return jnp.where((rolled < level) | diagonal[None, None], 1, 0).astype(jnp.int32)


def draw_positive_slot(key, part):
    half = CANDS // 2
    offset = jax.random.randint(jax.random.fold_in(key, 41), (EVENTS, 2, PAIRS), 0, half)
    side = jnp.arange(2, dtype=jnp.int32)[None, :, None]
    return ((1 - side) * half + offset).astype(jnp.int32)


def draw_anchor_live(key, part):
    devices = PAIRS // PAIRS_DEV
    jitter = jax.random.randint(jax.random.fold_in(key, 31), (EVENTS, 2, devices), 0, PAIRS_DEV // 8 + 1)
    place = (jnp.arange(EVENTS)[:, None, None] * 2 + jnp.arange(2)[None, :, None]) * devices + jnp.arange(devices)[None, None, :]
    final = max(EVENTS * 2 * devices - 1, 1)
    count = PAIRS_DEV // 3 + 2 * PAIRS_DEV // 3 * place // final - jitter
    count_rows = jnp.repeat(count, PAIRS_DEV, axis=2)
    position = jnp.arange(PAIRS) % PAIRS_DEV
    return (position[None, None, :] < count_rows).astype(jnp.int32)


def set_ends(entries, stream_key, low, high):
    longest = entries.shape.index(max(entries.shape))
    spots = []
    for shift in (0, 1):
        where = [jax.random.randint(jax.random.fold_in(stream_key, axis), (), 0, length) for axis, length in enumerate(entries.shape)]
        where[longest] = (where[longest] + shift) % entries.shape[longest]
        spots.append(tuple(where))
    return entries.at[spots[0]].set(low).at[spots[1]].set(high)


def level_of(key, dims, pieces, least, high):
    factor_of = 1.0
    for axis_at, blocks in pieces:
        heights = jax.random.uniform(jax.random.fold_in(jax.random.fold_in(key, 6), axis_at), (blocks,), jnp.float32, least / len(pieces), high / len(pieces))
        factor_of = factor_of * jnp.repeat(jnp.exp(heights), dims[axis_at] // blocks).reshape((-1,) + (1,) * (len(dims) - 1 - axis_at))
    return factor_of


def bell_draw(own_key, dims, deviation, reach, split=(), held_as=jnp.bfloat16):
    factor_of = level_of(own_key, dims, split, -0.22, 0.18) if split else 1.0
    entries = jax.random.normal(own_key, dims, jnp.float32) * deviation * factor_of
    return jnp.minimum(jnp.maximum(entries, -reach), reach).astype(held_as)


def setup_inputs(seed: int = 0) -> dict:
    seeds = jax.random.split(jax.random.key(seed), 10)
    return {
        "query": draw_query(jax.random.fold_in(seeds[9], 71), 0),
        "key": draw_key(jax.random.fold_in(seeds[9], 71), 0),
        "value": bell_draw(seeds[2], (EVENTS, 2, NPTS, D), 1.0, 6.0, ((0, 4), (1, 2), (2, 4))),
        "pattern": draw_pattern(jax.random.fold_in(seeds[9], 71), 0),
        "out_weight": bell_draw(seeds[4], (D, D), D ** -0.5, 0.25),
        "served": set_ends(jax.random.randint(seeds[5], (EVENTS, 2, REQS, CAP), 0, PTS_DEV), jax.random.fold_in(seeds[5], 1), 0, PTS_DEV - 1).astype(jnp.int32),
        "anchor_rows": set_ends(jax.random.randint(seeds[6], (EVENTS, 2, PAIRS), 0, PTS_DEV), jax.random.fold_in(seeds[6], 1), 0, PTS_DEV - 1).astype(jnp.int32),
        "positive_slot": draw_positive_slot(jax.random.fold_in(seeds[9], 71), 0),
        "anchor_live": draw_anchor_live(jax.random.fold_in(seeds[9], 71), 0),
    }


NEGATIVE = -1e+30
SHARPNESS_SCALE = 0.07

def attend_view(queries, keys, values, blocks):
    head_dim = D // HEADS
    scale = head_dim ** (-0.5)
    head_keys = keys.astype(jnp.float32).reshape(NPTS, HEADS, head_dim)
    head_values = values.astype(jnp.float32).reshape(NPTS, HEADS, head_dim)
    span = 4 * BLOCK
    key_block = jnp.arange(NPTS, dtype=jnp.int32) // BLOCK

    def one_block(index):
        query_rows = lax.dynamic_slice_in_dim(queries, index * span, span, 0).astype(jnp.float32).reshape(span, HEADS, head_dim)
        pattern_rows = lax.dynamic_slice_in_dim(blocks, index * 4, 4, 0)
        allowed = jnp.repeat(pattern_rows, BLOCK, axis=0)[:, key_block] > 0
        scores = jnp.einsum('qhd,khd->hqk', query_rows, head_keys, precision=lax.Precision.HIGHEST) * scale
        scores = jnp.where(allowed[None], scores, NEGATIVE)
        highest = lax.optimization_barrier(jnp.max(scores, axis=-1, keepdims=True))
        weights = jnp.where(allowed[None], jnp.exp(scores - highest), 0.0)
        totals = lax.optimization_barrier(jnp.sum(weights, axis=-1))
        rounded = lax.optimization_barrier(weights.astype(jnp.bfloat16)).astype(jnp.float32)
        mixed = jnp.einsum('hqk,khd->qhd', rounded, head_values, precision=lax.Precision.HIGHEST) / totals.T[:, :, None]
        return mixed.reshape(span, D).astype(jnp.bfloat16)
    return lax.map(one_block, jnp.arange(NPTS // span, dtype=jnp.int32)).reshape(NPTS, D)

def reference(query, key, value, pattern, out_weight, served, anchor_rows, positive_slot, anchor_live):
    anchor_weight = out_weight.astype(jnp.float32)

    def event_step(carry, inputs):
        grad_sum, loss_sum, live_sum = carry
        queries, keys, values, blocks, served_rows, own_rows, positive, live_mask = inputs
        mixed = jnp.stack([attend_view(queries[0], keys[0], values[0], blocks[0]), attend_view(queries[1], keys[1], values[1], blocks[1])])
        embedding_rows = jnp.einsum('kxs,sf->kxf', mixed.astype(jnp.float32), anchor_weight, precision=lax.Precision.HIGHEST)
        inverse = lax.rsqrt(lax.optimization_barrier(jnp.sum(embedding_rows * embedding_rows, axis=-1)) + 1e-06)
        unit = (embedding_rows * inverse[..., None]).astype(jnp.bfloat16)
        owner_rows = jnp.arange(N_SEQ, dtype=jnp.int32)[:, None, None] * PTS_DEV + served_rows.reshape(2, N_SEQ, 2 * N_SEQ, CAP)
        picked = jnp.stack([unit[0][owner_rows[0]], unit[1][owner_rows[1]]])
        contender_vectors = picked.transpose(2, 0, 1, 3, 4).reshape(2 * N_SEQ, CANDS, D).astype(jnp.float32)
        anchor_index = jnp.arange(PAIRS, dtype=jnp.int32) // PAIRS_DEV * PTS_DEV + own_rows
        query_vectors = jnp.stack([unit[0][anchor_index[0]], unit[1][anchor_index[1]]])
        query_vectors = query_vectors.reshape(2 * N_SEQ, PAIRS_DEV, D).astype(jnp.float32)
        pairwise_scores = jnp.einsum('ftg,fyg->fty', query_vectors, contender_vectors, precision=lax.Precision.HIGHEST) / SHARPNESS_SCALE
        exponentiated_scores = jnp.exp(pairwise_scores)
        partition_totals = lax.optimization_barrier(jnp.sum(exponentiated_scores, axis=-1))
        log_total = jnp.log(partition_totals)
        correct_column = (jnp.arange(CANDS, dtype=jnp.int32)[None, None, :] == positive.reshape(2 * N_SEQ, PAIRS_DEV)[..., None]).astype(jnp.float32)
        active_queries = live_mask.reshape(2 * N_SEQ, PAIRS_DEV).astype(jnp.float32)
        loss_sum = loss_sum + jnp.sum(active_queries * (log_total - lax.optimization_barrier(jnp.sum(pairwise_scores * correct_column, axis=-1))))
        live_sum = live_sum + jnp.sum(active_queries)
        score_derivatives = active_queries[..., None] * (exponentiated_scores / partition_totals[..., None] - correct_column) / SHARPNESS_SCALE
        anchor_grads = jnp.einsum('rak,rkd->rad', score_derivatives, contender_vectors, precision=lax.Precision.HIGHEST).reshape(2, PAIRS, D)
        candidate_grads = jnp.einsum('rak,rad->rkd', score_derivatives, query_vectors, precision=lax.Precision.HIGHEST)
        candidate_grads = candidate_grads.reshape(2 * N_SEQ, 2, N_SEQ, CAP, D).transpose(1, 2, 0, 3, 4)
        gathered = []
        for side in range(2):
            grads = jnp.zeros((NPTS, D), jnp.float32).at[owner_rows[side].reshape(-1)].add(candidate_grads[side].reshape(-1, D))
            grads = grads.at[anchor_index[side]].add(anchor_grads[side])
            gathered.append(grads)
        unit_grads = jnp.stack(gathered)
        inner = lax.optimization_barrier(jnp.sum(embedding_rows * unit_grads, axis=-1))
        embedding_gradients = (inverse[..., None] * (unit_grads - embedding_rows * (inverse * inverse * inner)[..., None])).astype(jnp.bfloat16)
        loss_term = jnp.einsum('guh,guy->hy', mixed.astype(jnp.float32), embedding_gradients.astype(jnp.float32), precision=lax.Precision.HIGHEST)
        return ((grad_sum + loss_term, loss_sum, live_sum), mixed)
    start = (jnp.zeros((D, D), jnp.float32), jnp.zeros((), jnp.float32), jnp.zeros((), jnp.float32))
    finals, mixed = lax.scan(event_step, start, (query, key, value, pattern, served, anchor_rows, positive_slot, anchor_live))
    grad_total, loss_total, live_total = finals
    return (mixed, grad_total, loss_total / live_total)
```

```python
import functools
import math

import jax
import jax.numpy as jnp
from jax import lax
from jax.experimental import pallas as pl
from jax.experimental.pallas import tpu as pltpu
from jax.sharding import PartitionSpec as P

HEADS = 16
BLOCK = 128
GROUP = 128
NEGATIVE = -1e30
SHARPNESS_SCALE = 0.07
F32 = jnp.float32
BF16 = jnp.bfloat16


def remote(src, dst, send, recv, device):
    return pltpu.make_async_remote_copy(
        src_ref=src,
        dst_ref=dst,
        send_sem=send,
        recv_sem=recv,
        device_id=device,
        device_id_type=pl.DeviceIdType.MESH,
    )


def greet(devices):
    barrier = pltpu.get_barrier_semaphore()
    for device in devices:
        pl.semaphore_signal(
            barrier, inc=1, device_id=device, device_id_type=pl.DeviceIdType.MESH
        )
    pl.semaphore_wait(barrier, len(devices))


def attention_kernel(
    n_seq, head_dim, pattern, q_ref, k_ref, v_ref, mixed_ref,
    k_all, v_all, q_wide, best, total, accum,
    mate_send, mate_recv, row_send, row_recv, pass_send, pass_recv,
):
    points, width = q_ref.shape
    blocks = points // BLOCK
    groups = width // GROUP
    per_group = GROUP // head_dim
    rows = n_seq // 2
    me = lax.axis_index("seq")
    my_row, core = me // 2, me % 2
    mate = my_row * 2 + 1 - core
    mate_id = {"seq": mate}

    def row_peer(step):
        return lax.rem(my_row + step, rows) * 2 + core

    def row_source(step):
        return lax.rem(my_row + rows - step, rows)

    greet([mate_id] + [{"seq": row_peer(step)} for step in range(1, rows)])

    def key_row_copy(step, i):
        place = pl.ds(pl.multiple_of(i * BLOCK, BLOCK), BLOCK)
        return remote(
            k_ref.at[place], k_all.at[me, place],
            row_send.at[step - 1, 0, i], row_recv.at[step - 1, 0, i],
            {"seq": row_peer(step)},
        )

    def value_row_copy(step, i):
        return remote(
            v_all.at[me, i], v_all.at[me, i],
            row_send.at[step - 1, 1, i], row_recv.at[step - 1, 1, i],
            {"seq": row_peer(step)},
        )

    key_mate = remote(k_ref, k_all.at[me], mate_send.at[0], mate_recv.at[0], mate_id)
    value_mate = remote(
        v_all.at[me], v_all.at[me], mate_send.at[1], mate_recv.at[1], mate_id
    )

    key_row_copy(1, 0).start()
    for i in range(blocks):
        v_all[me, i] = v_ref[i * BLOCK : (i + 1) * BLOCK, :].T
        for step in range(1, rows):
            if step > 1 or i > 0:
                key_row_copy(step, i).start()
            value_row_copy(step, i).start()
    key_mate.start()
    value_mate.start()
    k_all[me] = k_ref[...]

    factor_in = head_dim ** (-0.5) * math.log2(math.e)
    q_wide[...] = jnp.zeros_like(q_wide)
    for b in range(blocks):
        turned = q_ref[b * BLOCK : (b + 1) * BLOCK, :].T.astype(F32) * factor_in
        high = turned.astype(BF16)
        low = (turned - high.astype(F32)).astype(BF16)
        for g in range(groups):
            for j in range(per_group):
                at = g * GROUP + j * head_dim
                cols = slice(j * BLOCK, (j + 1) * BLOCK)
                q_wide[b, g, j * head_dim : (j + 1) * head_dim, cols] = high[at : at + head_dim]
                q_wide[b, g, GROUP + j * head_dim : GROUP + (j + 1) * head_dim, cols] = low[
                    at : at + head_dim
                ]
    best[...] = jnp.full_like(best, NEGATIVE)
    total[...] = jnp.zeros_like(total)
    accum[...] = jnp.zeros_like(accum)

    def attend(source, i):
        place = pl.ds(pl.multiple_of(i * BLOCK, BLOCK), BLOCK)

        def one(b, carry):
            keep = pattern[b, source * blocks + i].astype(F32)
            bias = (keep - 1.0) * (-NEGATIVE)
            for g in range(groups):
                lanes = slice(g * GROUP, (g + 1) * GROUP)
                keys = k_all[source, place, lanes]
                scores = jnp.dot(
                    jnp.concatenate([keys, keys], axis=1), q_wide[b, g],
                    preferred_element_type=F32,
                )
                top = jnp.max(scores, axis=0, keepdims=True)
                old = best[b, g : g + 1]
                new = jnp.maximum(old, top + bias)
                weights = jnp.exp2(scores - jnp.maximum(old, top)).astype(BF16)
                fade = jnp.exp2(old - new)
                vals = v_all[source, i, lanes, :]
                vals = jnp.concatenate([vals, jnp.ones((16, BLOCK), BF16)], axis=0)
                vals = vals * keep.astype(BF16)
                out = jnp.dot(vals, weights, preferred_element_type=F32)
                best[b, g : g + 1] = new
                total[b, g : g + 1] = total[b, g : g + 1] * fade + out[GROUP : GROUP + 1]
                for j in range(per_group):
                    cols = slice(j * BLOCK, (j + 1) * BLOCK)
                    at = g * GROUP + j * head_dim
                    accum[b, at : at + head_dim] = (
                        accum[b, at : at + head_dim] * fade[:, cols]
                        + out[j * head_dim : (j + 1) * head_dim, cols]
                    )
            return carry

        lax.fori_loop(0, blocks, one, 0)

    lax.fori_loop(0, blocks, lambda i, c: (attend(me, i), c)[1], 0)
    remote(k_ref, k_all.at[mate], mate_send.at[0], mate_recv.at[0], mate_id).wait_recv()
    remote(
        v_all.at[mate], v_all.at[mate], mate_send.at[1], mate_recv.at[1], mate_id
    ).wait_recv()
    lax.fori_loop(0, blocks, lambda i, c: (attend(mate, i), c)[1], 0)

    for step in range(1, rows):
        origin = row_source(step) * 2
        near, far = origin + core, origin + 1 - core

        def arriving(i, carry, step=step, near=near, far=far):
            place = pl.ds(pl.multiple_of(i * BLOCK, BLOCK), BLOCK)
            remote(
                k_ref.at[place], k_all.at[near, place],
                row_send.at[step - 1, 0, i], row_recv.at[step - 1, 0, i], mate_id,
            ).wait_recv()
            remote(
                k_all.at[near, place], k_all.at[near, place],
                pass_send.at[step - 1, 0, i], pass_recv.at[step - 1, 0, i], mate_id,
            ).start()
            remote(
                v_all.at[near, i], v_all.at[near, i],
                row_send.at[step - 1, 1, i], row_recv.at[step - 1, 1, i], mate_id,
            ).wait_recv()
            remote(
                v_all.at[near, i], v_all.at[near, i],
                pass_send.at[step - 1, 1, i], pass_recv.at[step - 1, 1, i], mate_id,
            ).start()
            attend(near, i)
            remote(
                k_all.at[far, place], k_all.at[far, place],
                pass_send.at[step - 1, 0, i], pass_recv.at[step - 1, 0, i], mate_id,
            ).wait_recv()
            remote(
                v_all.at[far, i], v_all.at[far, i],
                pass_send.at[step - 1, 1, i], pass_recv.at[step - 1, 1, i], mate_id,
            ).wait_recv()
            attend(far, i)
            return carry

        lax.fori_loop(0, blocks, arriving, 0)

    for b in range(blocks):
        for g in range(groups):
            parts = []
            for j in range(per_group):
                at = g * GROUP + j * head_dim
                cols = slice(j * BLOCK, (j + 1) * BLOCK)
                parts.append(accum[b, at : at + head_dim] / total[b, g : g + 1, cols])
            mixed_ref[b * BLOCK : (b + 1) * BLOCK, g * GROUP : (g + 1) * GROUP] = (
                jnp.concatenate(parts, axis=0).T.astype(BF16)
            )

    key_mate.wait_send()
    value_mate.wait_send()
    for step in range(1, rows):
        near = row_source(step) * 2 + core
        for i in range(blocks):
            place = slice(i * BLOCK, (i + 1) * BLOCK)
            key_row_copy(step, i).wait_send()
            value_row_copy(step, i).wait_send()
            remote(
                k_all.at[near, place], k_all.at[near, place],
                pass_send.at[step - 1, 0, i], pass_recv.at[step - 1, 0, i], mate_id,
            ).wait_send()
            remote(
                v_all.at[near, i], v_all.at[near, i],
                pass_send.at[step - 1, 1, i], pass_recv.at[step - 1, 1, i], mate_id,
            ).wait_send()


def attention(pattern, queries, keys, values, n_seq):
    points, width = queries.shape
    head_dim = width // HEADS
    blocks = points // BLOCK
    groups = width // GROUP
    rows = n_seq // 2
    wide = GROUP // head_dim * BLOCK
    vmem = pl.BlockSpec(memory_space=pltpu.VMEM)
    hops = max(rows - 1, 1)
    return pl.pallas_call(
        functools.partial(attention_kernel, n_seq, head_dim),
        out_shape=jax.ShapeDtypeStruct((points, width), BF16),
        in_specs=[pl.BlockSpec(memory_space=pltpu.SMEM), vmem, vmem, vmem],
        out_specs=vmem,
        scratch_shapes=[
            pltpu.VMEM((n_seq, points, width), BF16),
            pltpu.VMEM((n_seq, blocks, width, BLOCK), BF16),
            pltpu.VMEM((blocks, groups, 2 * GROUP, wide), BF16),
            pltpu.VMEM((blocks, groups, wide), F32),
            pltpu.VMEM((blocks, groups, wide), F32),
            pltpu.VMEM((blocks, width, BLOCK), F32),
            pltpu.SemaphoreType.DMA((2,)),
            pltpu.SemaphoreType.DMA((2,)),
            pltpu.SemaphoreType.DMA((hops, 2, blocks)),
            pltpu.SemaphoreType.DMA((hops, 2, blocks)),
            pltpu.SemaphoreType.DMA((hops, 2, blocks)),
            pltpu.SemaphoreType.DMA((hops, 2, blocks)),
        ],
        compiler_params=pltpu.CompilerParams(
            collective_id=0, has_side_effects=True, vmem_limit_bytes=48 * 1024 * 1024
        ),
    )(pattern, queries, keys, values)


def contrast_kernel(
    n_seq, n_plane, n_event,
    mixed_ref, weight_ref, served_ref, rows_ref, slot_ref, live_ref,
    grad_ref, loss_ref,
    embed, outgoing, contenders, picks, logits, back_out, back_in,
    part_out, part_in, event_all, whole_all, plane_stat, event_stat,
    go_send, go_recv, back_send, back_recv, part_send, part_recv,
    event_send, event_recv, whole_send, whole_recv,
    pstat_send, pstat_recv, estat_send, estat_recv,
):
    points, width = mixed_ref.shape
    capacity = served_ref.shape[1]
    anchors_dev = rows_ref.shape[1]
    chunk = part_out.shape[1]
    me = lax.axis_index("view") * n_seq + lax.axis_index("seq")
    my_event = lax.axis_index("event")

    def plane_id(peer):
        return {"view": peer // n_seq, "seq": lax.rem(peer, n_seq)}

    def peer_at(step):
        return lax.rem(me + step, n_plane)

    def event_at(step):
        return lax.rem(my_event + step, n_event)

    greet(
        [plane_id(peer_at(step)) for step in range(1, n_plane)]
        + [{"event": event_at(step)} for step in range(1, n_event)]
    )
    others = [n_plane - step for step in range(1, n_plane)]

    def swap(src, dst, send, recv, peer, slot):
        return remote(src, dst.at[slot], send.at[peer], recv.at[slot], plane_id(peer))

    mixed = mixed_ref[...]
    embed[...] = jnp.dot(mixed, weight_ref[...], preferred_element_type=F32)
    rows = embed[...]
    inverse = lax.rsqrt(jnp.sum(rows * rows, axis=-1, keepdims=True) + 1e-06)
    unit = (rows * inverse).astype(BF16)

    point_index = lax.broadcasted_iota(jnp.int32, (points, capacity), 0)

    def pick_of(peer):
        return jnp.where(served_ref[pl.ds(peer, 1), :] == point_index, 1.0, 0.0)

    def gather(peer):
        pick = pick_of(peer).astype(BF16)
        picks[peer] = pick
        return jnp.dot(pick.T, unit, preferred_element_type=F32).astype(BF16)

    for step in others:
        peer = peer_at(step)
        outgoing[peer] = gather(peer)
        swap(outgoing.at[peer], contenders, go_send, go_recv, peer, me).start()
    contenders[me] = gather(me)

    anchor_pick = jnp.where(
        rows_ref[...] == lax.broadcasted_iota(jnp.int32, (points, anchors_dev), 0), 1.0, 0.0
    ).astype(BF16)
    anchors = jnp.dot(anchor_pick.T, unit, preferred_element_type=F32).astype(BF16)
    mixed_turned = mixed.T
    live = live_ref[...].astype(F32)
    slots = slot_ref[...]
    slot_index = lax.broadcasted_iota(jnp.int32, (capacity, anchors_dev), 0)

    def correct(peer):
        return jnp.where(slots - peer * capacity == slot_index, 1.0, 0.0)

    sums = jnp.zeros((1, anchors_dev), F32)
    goal = jnp.zeros((1, anchors_dev), F32)
    for step in [0] + [n_plane - s for s in others]:
        peer = peer_at(step)
        if step:
            swap(outgoing.at[peer], contenders, go_send, go_recv, peer, peer).wait_recv()
        scores = lax.dot_general(
            contenders[peer], anchors, (((1,), (1,)), ((), ())), preferred_element_type=F32
        ) / SHARPNESS_SCALE
        grown = jnp.exp(scores)
        logits[peer] = grown
        sums = sums + jnp.sum(grown, axis=0, keepdims=True)
        goal = goal + jnp.sum(scores * correct(peer), axis=0, keepdims=True)
    loss_part = jnp.sum(live * (jnp.log(sums) - goal), axis=1, keepdims=True)
    live_part = jnp.sum(live, axis=1, keepdims=True)
    row_index = lax.broadcasted_iota(jnp.int32, (8, 128), 0)
    plane_stat[me] = jnp.where(row_index == 0, loss_part, live_part)

    def grads_of(peer):
        return live * (logits[peer] / sums - correct(peer)) / SHARPNESS_SCALE

    def answer(peer):
        slopes = grads_of(peer).astype(BF16)
        return jnp.dot(slopes, anchors, preferred_element_type=F32).astype(BF16), slopes

    anchor_grads = jnp.zeros((anchors_dev, width), F32)
    for step in others:
        peer = peer_at(step)
        reply, slopes = answer(peer)
        back_out[peer] = reply
        swap(back_out.at[peer], back_in, back_send, back_recv, peer, me).start()
        swap(plane_stat.at[me], plane_stat, pstat_send, pstat_recv, peer, me).start()
        anchor_grads = anchor_grads + jnp.dot(
            slopes.T, contenders[peer], preferred_element_type=F32
        )
    reply, slopes = answer(me)
    back_in[me] = reply
    anchor_grads = anchor_grads + jnp.dot(slopes.T, contenders[me], preferred_element_type=F32)
    high = anchor_grads.astype(BF16)
    low = (anchor_grads - high.astype(F32)).astype(BF16)
    unit_grads = (
        jnp.dot(anchor_pick, high, preferred_element_type=F32)
        + jnp.dot(anchor_pick, low, preferred_element_type=F32)
        + jnp.dot(picks[me], back_in[me], preferred_element_type=F32)
    )
    for step in [n_plane - s for s in others]:
        peer = peer_at(step)
        swap(back_out.at[peer], back_in, back_send, back_recv, peer, peer).wait_recv()
        unit_grads = unit_grads + jnp.dot(
            picks[peer], back_in[peer], preferred_element_type=F32
        )
    rows = embed[...]
    inner = jnp.sum(rows * unit_grads, axis=-1, keepdims=True)
    embed_grads = (
        inverse * (unit_grads - rows * (inverse * inverse * inner))
    ).astype(BF16)
    part = jnp.dot(mixed_turned, embed_grads, preferred_element_type=F32).astype(BF16)
    for p in range(n_plane):
        part_out[p] = part[p * chunk : (p + 1) * chunk]

    for step in others:
        peer = peer_at(step)
        swap(part_out.at[peer], part_in, part_send, part_recv, peer, me).start()
    part_in[me] = part_out[me]
    for step in range(1, n_plane):
        peer = peer_at(step)
        swap(plane_stat.at[me], plane_stat, pstat_send, pstat_recv, peer, peer).wait_recv()
    stat = plane_stat[0]
    for p in range(1, n_plane):
        stat = stat + plane_stat[p]
    event_stat[my_event] = stat

    def event_swap(array, send, recv, step, slot):
        event = event_at(step)
        return remote(
            array.at[my_event], array.at[slot], send.at[event], recv.at[slot], {"event": event}
        )

    for step in range(1, n_event):
        event_swap(event_stat, estat_send, estat_recv, step, my_event).start()
    for step in range(1, n_plane):
        peer = peer_at(step)
        swap(part_out.at[peer], part_in, part_send, part_recv, peer, peer).wait_recv()
    reduced = part_in[0].astype(F32)
    for p in range(1, n_plane):
        reduced = reduced + part_in[p].astype(F32)
    event_all[my_event] = reduced.astype(BF16)
    for step in range(1, n_event):
        event_swap(event_all, event_send, event_recv, step, my_event).start()
    for step in range(1, n_event):
        event_swap(event_stat, estat_send, estat_recv, step, event_at(step)).wait_recv()
        event_swap(event_all, event_send, event_recv, step, event_at(step)).wait_recv()
    reduced = event_all[0].astype(F32)
    stat = event_stat[0]
    for e in range(1, n_event):
        reduced = reduced + event_all[e].astype(F32)
        stat = stat + event_stat[e]
    whole_all[me] = reduced.astype(BF16)
    for step in others:
        peer = peer_at(step)
        swap(whole_all.at[me], whole_all, whole_send, whole_recv, peer, me).start()
    loss_ref[0, 0] = jnp.max(stat[0:1] / stat[1:2])

    def unpack(p):
        grad_ref[pl.ds(pl.multiple_of(p * chunk, chunk), chunk), :] = whole_all[p].astype(F32)

    unpack(me)
    for step in [n_plane - s for s in others]:
        peer = peer_at(step)
        swap(whole_all.at[me], whole_all, whole_send, whole_recv, peer, peer).wait_recv()
        unpack(peer)

    for step in others:
        peer = peer_at(step)
        swap(outgoing.at[peer], contenders, go_send, go_recv, peer, me).wait_send()
        swap(back_out.at[peer], back_in, back_send, back_recv, peer, me).wait_send()
        swap(plane_stat.at[me], plane_stat, pstat_send, pstat_recv, peer, me).wait_send()
        swap(part_out.at[peer], part_in, part_send, part_recv, peer, me).wait_send()
        swap(whole_all.at[me], whole_all, whole_send, whole_recv, peer, me).wait_send()
    for step in range(1, n_event):
        event_swap(event_stat, estat_send, estat_recv, step, my_event).wait_send()
        event_swap(event_all, event_send, event_recv, step, my_event).wait_send()


def contrast(mixed, out_weight, served, rows, slots, live, n_seq, n_plane, n_event):
    points, width = mixed.shape
    senders, capacity = served.shape
    anchors_dev = rows.shape[1]
    chunk = width // n_plane
    vmem = pl.BlockSpec(memory_space=pltpu.VMEM)
    plane_sems = pltpu.SemaphoreType.DMA((n_plane,))
    event_sems = pltpu.SemaphoreType.DMA((n_event,))
    return pl.pallas_call(
        functools.partial(contrast_kernel, n_seq, n_plane, n_event),
        out_shape=(
            jax.ShapeDtypeStruct((width, width), F32),
            jax.ShapeDtypeStruct((1, 1), F32),
        ),
        in_specs=[vmem] * 6,
        out_specs=(vmem, pl.BlockSpec(memory_space=pltpu.SMEM)),
        scratch_shapes=[
            pltpu.VMEM((points, width), F32),
            pltpu.VMEM((senders, capacity, width), BF16),
            pltpu.VMEM((senders, capacity, width), BF16),
            pltpu.VMEM((senders, points, capacity), BF16),
            pltpu.VMEM((senders, capacity, anchors_dev), F32),
            pltpu.VMEM((senders, capacity, width), BF16),
            pltpu.VMEM((senders, capacity, width), BF16),
            pltpu.VMEM((n_plane, chunk, width), BF16),
            pltpu.VMEM((n_plane, chunk, width), BF16),
            pltpu.VMEM((n_event, chunk, width), BF16),
            pltpu.VMEM((n_plane, chunk, width), BF16),
            pltpu.VMEM((n_plane, 8, 128), F32),
            pltpu.VMEM((n_event, 8, 128), F32),
        ]
        + [plane_sems] * 6
        + [event_sems] * 2
        + [plane_sems] * 4
        + [event_sems] * 2,
        compiler_params=pltpu.CompilerParams(
            collective_id=1, has_side_effects=True, vmem_limit_bytes=48 * 1024 * 1024
        ),
    )(mixed, out_weight, served, rows, slots, live)


def per_device(
    query, key, value, pattern, out_weight, served, anchor_rows, positive_slot, anchor_live
):
    n_view, n_seq, n_event = (lax.axis_size(name) for name in ("view", "seq", "event"))
    mixed = attention(pattern[0, 0], query[0, 0], key[0, 0], value[0, 0], n_seq)
    grad, loss = contrast(
        mixed, out_weight, served[0, 0], anchor_rows[0], positive_slot[0], anchor_live[0],
        n_seq, n_view * n_seq, n_event,
    )
    return (mixed[None, None], grad, loss[0, 0])


def solution(mesh):
    placed = (
        P("event", "view", "seq", None),
        P("event", "view", "seq", None),
        P("event", "view", "seq", None),
        P("event", "view", "seq", None),
        P(),
        P("event", "view", "seq", None),
        P("event", "view", "seq"),
        P("event", "view", "seq"),
        P("event", "view", "seq"),
    )
    return jax.shard_map(
        per_device,
        mesh=mesh,
        in_specs=placed,
        out_specs=(P("event", "view", "seq", None), P(), P()),
        check_vma=False,
    )
```

```python
import functools
import math

import jax
import jax.numpy as jnp
from jax import lax
from jax.experimental import pallas as pl
from jax.experimental.pallas import tpu as pltpu
from jax.sharding import PartitionSpec as P

HEADS = 16
BLOCK = 128
GROUP = 128
NEGATIVE = -1e30
SHARPNESS_SCALE = 0.07
F32 = jnp.float32
BF16 = jnp.bfloat16


def remote(src, dst, send, recv, device):
    return pltpu.make_async_remote_copy(
        src_ref=src,
        dst_ref=dst,
        send_sem=send,
        recv_sem=recv,
        device_id=device,
        device_id_type=pl.DeviceIdType.MESH,
    )


def greet(devices):
    barrier = pltpu.get_barrier_semaphore()
    for device in devices:
        pl.semaphore_signal(
            barrier, inc=1, device_id=device, device_id_type=pl.DeviceIdType.MESH
        )
    pl.semaphore_wait(barrier, len(devices))


def attention_kernel(
    n_seq, head_dim, pattern, q_ref, k_ref, v_ref, mixed_ref,
    k_all, v_all, q_wide, best, total, accum,
    mate_send, mate_recv, row_send, row_recv, pass_send, pass_recv,
):
    points, width = q_ref.shape
    blocks = points // BLOCK
    groups = width // GROUP
    per_group = GROUP // head_dim
    rows = n_seq // 2
    me = lax.axis_index("seq")
    my_row, core = me // 2, me % 2
    mate = my_row * 2 + 1 - core
    mate_id = {"seq": mate}

    def row_peer(step):
        return lax.rem(my_row + step, rows) * 2 + core

    def row_source(step):
        return lax.rem(my_row + rows - step, rows)

    greet([mate_id] + [{"seq": row_peer(step)} for step in range(1, rows)])

    def key_row_copy(step, i):
        place = pl.ds(pl.multiple_of(i * BLOCK, BLOCK), BLOCK)
        return remote(
            k_ref.at[place], k_all.at[me, place],
            row_send.at[step - 1, 0, i], row_recv.at[step - 1, 0, i],
            {"seq": row_peer(step)},
        )

    def value_row_copy(step, i):
        return remote(
            v_all.at[me, i], v_all.at[me, i],
            row_send.at[step - 1, 1, i], row_recv.at[step - 1, 1, i],
            {"seq": row_peer(step)},
        )

    key_mate = remote(k_ref, k_all.at[me], mate_send.at[0], mate_recv.at[0], mate_id)
    value_mate = remote(
        v_all.at[me], v_all.at[me], mate_send.at[1], mate_recv.at[1], mate_id
    )

    key_row_copy(1, 0).start()
    for i in range(blocks):
        v_all[me, i] = v_ref[i * BLOCK : (i + 1) * BLOCK, :].T
        for step in range(1, rows):
            if step > 1 or i > 0:
                key_row_copy(step, i).start()
            value_row_copy(step, i).start()
    key_mate.start()
    value_mate.start()
    k_all[me] = k_ref[...]

    factor_in = head_dim ** (-0.5) * math.log2(math.e)
    q_wide[...] = jnp.zeros_like(q_wide)
    for b in range(blocks):
        turned = q_ref[b * BLOCK : (b + 1) * BLOCK, :].T.astype(F32) * factor_in
        high = turned.astype(BF16)
        low = (turned - high.astype(F32)).astype(BF16)
        for g in range(groups):
            for j in range(per_group):
                at = g * GROUP + j * head_dim
                cols = slice(j * BLOCK, (j + 1) * BLOCK)
                q_wide[b, g, j * head_dim : (j + 1) * head_dim, cols] = high[at : at + head_dim]
                q_wide[b, g, GROUP + j * head_dim : GROUP + (j + 1) * head_dim, cols] = low[
                    at : at + head_dim
                ]
    best[...] = jnp.full_like(best, NEGATIVE)
    total[...] = jnp.zeros_like(total)
    accum[...] = jnp.zeros_like(accum)

    ones = jnp.ones((16, BLOCK), BF16)

    def attend(first, second, i):
        place = pl.ds(pl.multiple_of(i * BLOCK, BLOCK), BLOCK)
        sources = (first, second)
        keeps = [
            [pattern[b, source * blocks + i].astype(F32) for source in sources]
            for b in range(blocks)
        ]

        def scores_of(b, g):
            lanes = slice(g * GROUP, (g + 1) * GROUP)
            keys = jnp.concatenate([k_all[source, place, lanes] for source in sources], axis=0)
            return jnp.dot(
                jnp.concatenate([keys, keys], axis=1), q_wide[b, g], preferred_element_type=F32
            )

        def finish(b, g, scores):
            lanes = slice(g * GROUP, (g + 1) * GROUP)
            halves = [scores[:BLOCK], scores[BLOCK:]]
            tops = [jnp.max(half, axis=0, keepdims=True) for half in halves]
            old = best[b, g : g + 1]
            new = old
            for top, keep in zip(tops, keeps[b]):
                new = jnp.maximum(new, top + (keep - 1.0) * (-NEGATIVE))
            weights = jnp.concatenate(
                [
                    jnp.exp2(half - jnp.maximum(new, top)).astype(BF16)
                    for half, top in zip(halves, tops)
                ],
                axis=0,
            )
            fade = jnp.exp2(old - new)
            best[b, g : g + 1] = new
            vals = [
                jnp.concatenate([v_all[source, i, lanes, :], ones], axis=0) * keep.astype(BF16)
                for source, keep in zip(sources, keeps[b])
            ]
            vals = jnp.concatenate(vals, axis=1)
            pair = 2 * head_dim
            for n in range(per_group // 2):
                cols = slice(2 * n * BLOCK, (2 * n + 2) * BLOCK)
                rows_in = jnp.concatenate([vals[n * pair : (n + 1) * pair], vals[GROUP:]], axis=0)
                out = jnp.dot(rows_in, weights[:, cols], preferred_element_type=F32)
                total[b, g : g + 1, cols] = (
                    total[b, g : g + 1, cols] * fade[:, cols] + out[pair : pair + 1]
                )
                for j in range(2):
                    at = g * GROUP + (2 * n + j) * head_dim
                    side = slice(j * BLOCK, (j + 1) * BLOCK)
                    accum[b, at : at + head_dim] = (
                        accum[b, at : at + head_dim] * fade[:, cols][:, side]
                        + out[j * head_dim : (j + 1) * head_dim, side]
                    )

        units = [(b, g) for b in range(blocks) for g in range(groups)]
        ready = scores_of(*units[0])
        for at, unit in enumerate(units):
            later = scores_of(*units[at + 1]) if at + 1 < len(units) else None
            finish(*unit, ready)
            ready = later

    remote(k_ref, k_all.at[mate], mate_send.at[0], mate_recv.at[0], mate_id).wait_recv()
    remote(
        v_all.at[mate], v_all.at[mate], mate_send.at[1], mate_recv.at[1], mate_id
    ).wait_recv()
    lax.fori_loop(0, blocks, lambda i, c: (attend(me, mate, i), c)[1], 0)

    for step in range(1, rows):
        origin = row_source(step) * 2
        near, far = origin + core, origin + 1 - core

        def arriving(i, carry, step=step, near=near, far=far):
            place = pl.ds(pl.multiple_of(i * BLOCK, BLOCK), BLOCK)
            remote(
                k_ref.at[place], k_all.at[near, place],
                row_send.at[step - 1, 0, i], row_recv.at[step - 1, 0, i], mate_id,
            ).wait_recv()
            remote(
                k_all.at[near, place], k_all.at[near, place],
                pass_send.at[step - 1, 0, i], pass_recv.at[step - 1, 0, i], mate_id,
            ).start()
            remote(
                v_all.at[near, i], v_all.at[near, i],
                row_send.at[step - 1, 1, i], row_recv.at[step - 1, 1, i], mate_id,
            ).wait_recv()
            remote(
                v_all.at[near, i], v_all.at[near, i],
                pass_send.at[step - 1, 1, i], pass_recv.at[step - 1, 1, i], mate_id,
            ).start()
            remote(
                k_all.at[far, place], k_all.at[far, place],
                pass_send.at[step - 1, 0, i], pass_recv.at[step - 1, 0, i], mate_id,
            ).wait_recv()
            remote(
                v_all.at[far, i], v_all.at[far, i],
                pass_send.at[step - 1, 1, i], pass_recv.at[step - 1, 1, i], mate_id,
            ).wait_recv()
            attend(near, far, i)
            return carry

        lax.fori_loop(0, blocks, arriving, 0)

    for b in range(blocks):
        for g in range(groups):
            parts = []
            for j in range(per_group):
                at = g * GROUP + j * head_dim
                cols = slice(j * BLOCK, (j + 1) * BLOCK)
                parts.append(accum[b, at : at + head_dim] / total[b, g : g + 1, cols])
            mixed_ref[b * BLOCK : (b + 1) * BLOCK, g * GROUP : (g + 1) * GROUP] = (
                jnp.concatenate(parts, axis=0).T.astype(BF16)
            )

    key_mate.wait_send()
    value_mate.wait_send()
    for step in range(1, rows):
        near = row_source(step) * 2 + core
        for i in range(blocks):
            place = slice(i * BLOCK, (i + 1) * BLOCK)
            key_row_copy(step, i).wait_send()
            value_row_copy(step, i).wait_send()
            remote(
                k_all.at[near, place], k_all.at[near, place],
                pass_send.at[step - 1, 0, i], pass_recv.at[step - 1, 0, i], mate_id,
            ).wait_send()
            remote(
                v_all.at[near, i], v_all.at[near, i],
                pass_send.at[step - 1, 1, i], pass_recv.at[step - 1, 1, i], mate_id,
            ).wait_send()


def attention(pattern, queries, keys, values, n_seq):
    points, width = queries.shape
    head_dim = width // HEADS
    blocks = points // BLOCK
    groups = width // GROUP
    rows = n_seq // 2
    wide = GROUP // head_dim * BLOCK
    vmem = pl.BlockSpec(memory_space=pltpu.VMEM)
    hops = max(rows - 1, 1)
    return pl.pallas_call(
        functools.partial(attention_kernel, n_seq, head_dim),
        out_shape=jax.ShapeDtypeStruct((points, width), BF16),
        in_specs=[pl.BlockSpec(memory_space=pltpu.SMEM), vmem, vmem, vmem],
        out_specs=vmem,
        scratch_shapes=[
            pltpu.VMEM((n_seq, points, width), BF16),
            pltpu.VMEM((n_seq, blocks, width, BLOCK), BF16),
            pltpu.VMEM((blocks, groups, 2 * GROUP, wide), BF16),
            pltpu.VMEM((blocks, groups, wide), F32),
            pltpu.VMEM((blocks, groups, wide), F32),
            pltpu.VMEM((blocks, width, BLOCK), F32),
            pltpu.SemaphoreType.DMA((2,)),
            pltpu.SemaphoreType.DMA((2,)),
            pltpu.SemaphoreType.DMA((hops, 2, blocks)),
            pltpu.SemaphoreType.DMA((hops, 2, blocks)),
            pltpu.SemaphoreType.DMA((hops, 2, blocks)),
            pltpu.SemaphoreType.DMA((hops, 2, blocks)),
        ],
        compiler_params=pltpu.CompilerParams(
            collective_id=0, has_side_effects=True, vmem_limit_bytes=48 * 1024 * 1024
        ),
    )(pattern, queries, keys, values)


def contrast_kernel(
    n_seq, n_plane, n_event,
    mixed_ref, weight_ref, served_ref, rows_ref, slot_ref, live_ref,
    grad_ref, loss_ref,
    outgoing, contenders, direction, inverse, units, turned, logits, slopes, embed_grads,
    part_out, part_in, event_all, whole_all, plane_stat, event_stat,
    go_send, go_recv, part_send, part_recv,
    event_send, event_recv, whole_send, whole_recv,
    pstat_send, pstat_recv, estat_send, estat_recv,
):
    points, width = mixed_ref.shape
    capacity = served_ref.shape[1]
    anchors_dev = rows_ref.shape[1]
    chunk = part_out.shape[1]
    cands = n_plane * capacity
    me = lax.axis_index("view") * n_seq + lax.axis_index("seq")
    my_event = lax.axis_index("event")

    def plane_id(peer):
        return {"view": peer // n_seq, "seq": lax.rem(peer, n_seq)}

    def peer_at(step):
        return lax.rem(me + step, n_plane)

    def event_at(step):
        return lax.rem(my_event + step, n_event)

    greet(
        [plane_id(peer_at(step)) for step in range(1, n_plane)]
        + [{"event": event_at(step)} for step in range(1, n_event)]
    )
    others = [n_plane - step for step in range(1, n_plane)]

    def swap(src, dst, send, recv, peer, slot):
        return remote(src, dst.at[slot], send.at[peer], recv.at[slot], plane_id(peer))

    point_index = lax.broadcasted_iota(jnp.int32, (points, capacity), 0)

    def gather(peer):
        pick = jnp.where(served_ref[pl.ds(peer, 1), :] == point_index, 1.0, 0.0).astype(BF16)
        return jnp.dot(pick.T, mixed_ref[...], preferred_element_type=F32).astype(BF16)

    for step in others:
        peer = peer_at(step)
        outgoing[peer] = gather(peer)
        swap(outgoing.at[peer], contenders, go_send, go_recv, peer, me).start()
    contenders[me] = gather(me)

    anchor_pick = jnp.where(
        rows_ref[...] == lax.broadcasted_iota(jnp.int32, (points, anchors_dev), 0), 1.0, 0.0
    ).astype(BF16)
    anchor_mixed = jnp.dot(anchor_pick.T, mixed_ref[...], preferred_element_type=F32).astype(BF16)

    def project(rows_mixed, at):
        place = slice(at, at + rows_mixed.shape[0])
        embed = jnp.dot(rows_mixed, weight_ref[...], preferred_element_type=F32)
        scale = lax.rsqrt(jnp.sum(embed * embed, axis=-1, keepdims=True) + 1e-06)
        embed = embed * scale
        inverse[place] = scale
        direction[place] = embed
        units[place] = embed.astype(BF16)
        turned[:, place] = rows_mixed.T

    project(anchor_mixed, cands)
    anchors = units[cands:]
    live = live_ref[...].astype(F32)
    slots = slot_ref[...]
    slot_index = lax.broadcasted_iota(jnp.int32, (capacity, anchors_dev), 0)

    def correct(peer):
        return jnp.where(slots - peer * capacity == slot_index, 1.0, 0.0)

    sums = jnp.zeros((1, anchors_dev), F32)
    goal = jnp.zeros((1, anchors_dev), F32)
    arrivals = [0] + [n_plane - step for step in others]
    for at, step in enumerate(arrivals):
        peer = peer_at(step)
        if step:
            swap(outgoing.at[peer], contenders, go_send, go_recv, peer, peer).wait_recv()
        place = slice(at * capacity, (at + 1) * capacity)
        project(contenders[peer], at * capacity)
        scores = lax.dot_general(
            units[place], anchors, (((1,), (1,)), ((), ())), preferred_element_type=F32
        ) / SHARPNESS_SCALE
        grown = jnp.exp(scores)
        logits[place] = grown
        sums = sums + jnp.sum(grown, axis=0, keepdims=True)
        goal = goal + jnp.sum(scores * correct(peer), axis=0, keepdims=True)
    loss_part = jnp.sum(live * (jnp.log(sums) - goal), axis=1, keepdims=True)
    live_part = jnp.sum(live, axis=1, keepdims=True)
    row_index = lax.broadcasted_iota(jnp.int32, (8, 128), 0)
    plane_stat[me] = jnp.where(row_index == 0, loss_part, live_part)
    for step in others:
        peer = peer_at(step)
        swap(plane_stat.at[me], plane_stat, pstat_send, pstat_recv, peer, me).start()

    for at, step in enumerate(arrivals):
        place = slice(at * capacity, (at + 1) * capacity)
        slopes[place] = (
            live * (logits[place] / sums - correct(peer_at(step))) / SHARPNESS_SCALE
        ).astype(BF16)

    def pull_back(grads, place):
        along = direction[place]
        inner = jnp.sum(along * grads, axis=-1, keepdims=True)
        embed_grads[place] = (inverse[place] * (grads - along * inner)).astype(BF16)

    for at in range(0, cands, anchors_dev):
        place = slice(at, at + anchors_dev)
        pull_back(jnp.dot(slopes[place], anchors, preferred_element_type=F32), place)
    pull_back(
        jnp.dot(slopes[...].T, units[:cands], preferred_element_type=F32),
        slice(cands, cands + anchors_dev),
    )
    part = jnp.dot(turned[...], embed_grads[...], preferred_element_type=F32).astype(BF16)
    for p in range(n_plane):
        part_out[p] = part[p * chunk : (p + 1) * chunk]

    for step in others:
        peer = peer_at(step)
        swap(part_out.at[peer], part_in, part_send, part_recv, peer, me).start()
    part_in[me] = part_out[me]
    for step in range(1, n_plane):
        peer = peer_at(step)
        swap(plane_stat.at[me], plane_stat, pstat_send, pstat_recv, peer, peer).wait_recv()
    stat = plane_stat[0]
    for p in range(1, n_plane):
        stat = stat + plane_stat[p]
    event_stat[my_event] = stat

    def event_swap(array, send, recv, step, slot):
        event = event_at(step)
        return remote(
            array.at[my_event], array.at[slot], send.at[event], recv.at[slot], {"event": event}
        )

    for step in range(1, n_event):
        event_swap(event_stat, estat_send, estat_recv, step, my_event).start()
    for step in range(1, n_plane):
        peer = peer_at(step)
        swap(part_out.at[peer], part_in, part_send, part_recv, peer, peer).wait_recv()
    reduced = part_in[0].astype(F32)
    for p in range(1, n_plane):
        reduced = reduced + part_in[p].astype(F32)
    event_all[my_event] = reduced.astype(BF16)
    for step in range(1, n_event):
        event_swap(event_all, event_send, event_recv, step, my_event).start()
    for step in range(1, n_event):
        event_swap(event_stat, estat_send, estat_recv, step, event_at(step)).wait_recv()
        event_swap(event_all, event_send, event_recv, step, event_at(step)).wait_recv()
    reduced = event_all[0].astype(F32)
    stat = event_stat[0]
    for e in range(1, n_event):
        reduced = reduced + event_all[e].astype(F32)
        stat = stat + event_stat[e]
    whole_all[me] = reduced.astype(BF16)
    for step in others:
        peer = peer_at(step)
        swap(whole_all.at[me], whole_all, whole_send, whole_recv, peer, me).start()
    loss_ref[0, 0] = jnp.max(stat[0:1] / stat[1:2])

    def unpack(p):
        grad_ref[pl.ds(pl.multiple_of(p * chunk, chunk), chunk), :] = whole_all[p].astype(F32)

    unpack(me)
    for step in [n_plane - s for s in others]:
        peer = peer_at(step)
        swap(whole_all.at[me], whole_all, whole_send, whole_recv, peer, peer).wait_recv()
        unpack(peer)

    for step in others:
        peer = peer_at(step)
        swap(outgoing.at[peer], contenders, go_send, go_recv, peer, me).wait_send()
        swap(plane_stat.at[me], plane_stat, pstat_send, pstat_recv, peer, me).wait_send()
        swap(part_out.at[peer], part_in, part_send, part_recv, peer, me).wait_send()
        swap(whole_all.at[me], whole_all, whole_send, whole_recv, peer, me).wait_send()
    for step in range(1, n_event):
        event_swap(event_stat, estat_send, estat_recv, step, my_event).wait_send()
        event_swap(event_all, event_send, event_recv, step, my_event).wait_send()


def contrast(mixed, out_weight, served, rows, slots, live, n_seq, n_plane, n_event):
    points, width = mixed.shape
    senders, capacity = served.shape
    anchors_dev = rows.shape[1]
    chunk = width // n_plane
    cands = senders * capacity
    every = cands + anchors_dev
    vmem = pl.BlockSpec(memory_space=pltpu.VMEM)
    plane_sems = pltpu.SemaphoreType.DMA((n_plane,))
    event_sems = pltpu.SemaphoreType.DMA((n_event,))
    return pl.pallas_call(
        functools.partial(contrast_kernel, n_seq, n_plane, n_event),
        out_shape=(
            jax.ShapeDtypeStruct((width, width), F32),
            jax.ShapeDtypeStruct((1, 1), F32),
        ),
        in_specs=[vmem] * 6,
        out_specs=(vmem, pl.BlockSpec(memory_space=pltpu.SMEM)),
        scratch_shapes=[
            pltpu.VMEM((senders, capacity, width), BF16),
            pltpu.VMEM((senders, capacity, width), BF16),
            pltpu.VMEM((every, width), F32),
            pltpu.VMEM((every, 1), F32),
            pltpu.VMEM((every, width), BF16),
            pltpu.VMEM((width, every), BF16),
            pltpu.VMEM((cands, anchors_dev), F32),
            pltpu.VMEM((cands, anchors_dev), BF16),
            pltpu.VMEM((every, width), BF16),
            pltpu.VMEM((n_plane, chunk, width), BF16),
            pltpu.VMEM((n_plane, chunk, width), BF16),
            pltpu.VMEM((n_event, chunk, width), BF16),
            pltpu.VMEM((n_plane, chunk, width), BF16),
            pltpu.VMEM((n_plane, 8, 128), F32),
            pltpu.VMEM((n_event, 8, 128), F32),
        ]
        + [plane_sems] * 4
        + [event_sems] * 2
        + [plane_sems] * 4
        + [event_sems] * 2,
        compiler_params=pltpu.CompilerParams(
            collective_id=1, has_side_effects=True, vmem_limit_bytes=48 * 1024 * 1024
        ),
    )(mixed, out_weight, served, rows, slots, live)


def per_device(
    query, key, value, pattern, out_weight, served, anchor_rows, positive_slot, anchor_live
):
    n_view, n_seq, n_event = (lax.axis_size(name) for name in ("view", "seq", "event"))
    mixed = attention(pattern[0, 0], query[0, 0], key[0, 0], value[0, 0], n_seq)
    grad, loss = contrast(
        mixed, out_weight, served[0, 0], anchor_rows[0], positive_slot[0], anchor_live[0],
        n_seq, n_view * n_seq, n_event,
    )
    return (mixed[None, None], grad, loss[0, 0])


def solution(mesh):
    placed = (
        P("event", "view", "seq", None),
        P("event", "view", "seq", None),
        P("event", "view", "seq", None),
        P("event", "view", "seq", None),
        P(),
        P("event", "view", "seq", None),
        P("event", "view", "seq"),
        P("event", "view", "seq"),
        P("event", "view", "seq"),
    )
    return jax.shard_map(
        per_device,
        mesh=mesh,
        in_specs=placed,
        out_specs=(P("event", "view", "seq", None), P(), P()),
        check_vma=False,
    )
```

```python
import functools
import math

import jax
import jax.numpy as jnp
from jax import lax
from jax.experimental import pallas as pl
from jax.experimental.pallas import tpu as pltpu
from jax.sharding import PartitionSpec as P

HEADS = 16
BLOCK = 128
GROUP = 128
NEGATIVE = -1e30
SHARPNESS_SCALE = 0.07
F32 = jnp.float32
BF16 = jnp.bfloat16


def remote(src, dst, send, recv, device):
    return pltpu.make_async_remote_copy(
        src_ref=src,
        dst_ref=dst,
        send_sem=send,
        recv_sem=recv,
        device_id=device,
        device_id_type=pl.DeviceIdType.MESH,
    )


def greet(devices):
    barrier = pltpu.get_barrier_semaphore()
    for device in devices:
        pl.semaphore_signal(
            barrier, inc=1, device_id=device, device_id_type=pl.DeviceIdType.MESH
        )
    pl.semaphore_wait(barrier, len(devices))


def attention_kernel(
    n_seq, head_dim, pattern, q_ref, k_ref, v_ref, mixed_ref,
    q_in, v_in, k_all, v_all, q_wide, best, total, accum, load_sem,
    mate_send, mate_recv, row_send, row_recv, pass_send, pass_recv,
):
    points, width = q_ref.shape
    blocks = points // BLOCK
    groups = width // GROUP
    per_group = GROUP // head_dim
    rows = n_seq // 2
    me = lax.axis_index("seq")
    my_row, core = me // 2, me % 2
    mate = my_row * 2 + 1 - core
    mate_id = {"seq": mate}

    def row_peer(step):
        return lax.rem(my_row + step, rows) * 2 + core

    def row_source(step):
        return lax.rem(my_row + rows - step, rows)

    loads = [
        pltpu.make_async_copy(src, dst, load_sem.at[n])
        for n, (src, dst) in enumerate(((v_ref, v_in), (q_ref, q_in), (k_ref, k_all.at[me])))
    ]
    for load in loads:
        load.start()
    greet([mate_id] + [{"seq": row_peer(step)} for step in range(1, rows)])

    def key_row_copy(step, i):
        place = pl.ds(pl.multiple_of(i * BLOCK, BLOCK), BLOCK)
        return remote(
            k_ref.at[place], k_all.at[me, place],
            row_send.at[step - 1, 0, i], row_recv.at[step - 1, 0, i],
            {"seq": row_peer(step)},
        )

    def value_row_copy(step, i):
        return remote(
            v_all.at[me, i], v_all.at[me, i],
            row_send.at[step - 1, 1, i], row_recv.at[step - 1, 1, i],
            {"seq": row_peer(step)},
        )

    key_mate = remote(k_ref, k_all.at[me], mate_send.at[0], mate_recv.at[0], mate_id)
    value_mate = remote(
        v_all.at[me], v_all.at[me], mate_send.at[1], mate_recv.at[1], mate_id
    )

    key_row_copy(1, 0).start()
    loads[0].wait()
    for i in range(blocks):
        v_all[me, i] = v_in[i * BLOCK : (i + 1) * BLOCK, :].T
        for step in range(1, rows):
            if step > 1 or i > 0:
                key_row_copy(step, i).start()
            value_row_copy(step, i).start()
    key_mate.start()
    value_mate.start()
    loads[1].wait()
    factor_in = head_dim ** (-0.5) * math.log2(math.e)
    q_wide[...] = jnp.zeros_like(q_wide)
    for b in range(blocks):
        turned = q_in[b * BLOCK : (b + 1) * BLOCK, :].T.astype(F32) * factor_in
        high = turned.astype(BF16)
        low = (turned - high.astype(F32)).astype(BF16)
        for g in range(groups):
            for j in range(per_group):
                at = g * GROUP + j * head_dim
                cols = slice(j * BLOCK, (j + 1) * BLOCK)
                q_wide[b, g, j * head_dim : (j + 1) * head_dim, cols] = high[at : at + head_dim]
                q_wide[b, g, GROUP + j * head_dim : GROUP + (j + 1) * head_dim, cols] = low[
                    at : at + head_dim
                ]
    best[...] = jnp.full_like(best, NEGATIVE)
    total[...] = jnp.zeros_like(total)
    accum[...] = jnp.zeros_like(accum)

    ones = jnp.ones((16, BLOCK), BF16)

    def attend(first, second, i):
        place = pl.ds(pl.multiple_of(i * BLOCK, BLOCK), BLOCK)
        sources = (first, second)
        keeps = [
            [pattern[b, 0, source * blocks + i].astype(F32) for source in sources]
            for b in range(blocks)
        ]

        def scores_of(b, g):
            lanes = slice(g * GROUP, (g + 1) * GROUP)
            keys = jnp.concatenate([k_all[source, place, lanes] for source in sources], axis=0)
            return jnp.dot(
                jnp.concatenate([keys, keys], axis=1), q_wide[b, g], preferred_element_type=F32
            )

        def finish(b, g, scores):
            lanes = slice(g * GROUP, (g + 1) * GROUP)
            halves = [scores[:BLOCK], scores[BLOCK:]]
            tops = [jnp.max(half, axis=0, keepdims=True) for half in halves]
            old = best[b, g : g + 1]
            new = old
            for top, keep in zip(tops, keeps[b]):
                new = jnp.maximum(new, top + (keep - 1.0) * (-NEGATIVE))
            weights = jnp.concatenate(
                [
                    jnp.exp2(half - jnp.maximum(new, top)).astype(BF16)
                    for half, top in zip(halves, tops)
                ],
                axis=0,
            )
            fade = jnp.exp2(old - new)
            best[b, g : g + 1] = new
            vals = [
                jnp.concatenate([v_all[source, i, lanes, :], ones], axis=0) * keep.astype(BF16)
                for source, keep in zip(sources, keeps[b])
            ]
            vals = jnp.concatenate(vals, axis=1)
            pair = 2 * head_dim
            for n in range(per_group // 2):
                cols = slice(2 * n * BLOCK, (2 * n + 2) * BLOCK)
                rows_in = jnp.concatenate([vals[n * pair : (n + 1) * pair], vals[GROUP:]], axis=0)
                out = jnp.dot(rows_in, weights[:, cols], preferred_element_type=F32)
                total[b, g : g + 1, cols] = (
                    total[b, g : g + 1, cols] * fade[:, cols] + out[pair : pair + 1]
                )
                for j in range(2):
                    at = g * GROUP + (2 * n + j) * head_dim
                    side = slice(j * BLOCK, (j + 1) * BLOCK)
                    accum[b, at : at + head_dim] = (
                        accum[b, at : at + head_dim] * fade[:, cols][:, side]
                        + out[j * head_dim : (j + 1) * head_dim, side]
                    )

        units = [(b, g) for b in range(blocks) for g in range(groups)]
        ready = scores_of(*units[0])
        for at, unit in enumerate(units):
            later = scores_of(*units[at + 1]) if at + 1 < len(units) else None
            finish(*unit, ready)
            ready = later

    loads[2].wait()
    remote(k_ref, k_all.at[mate], mate_send.at[0], mate_recv.at[0], mate_id).wait_recv()
    remote(
        v_all.at[mate], v_all.at[mate], mate_send.at[1], mate_recv.at[1], mate_id
    ).wait_recv()
    lax.fori_loop(0, blocks, lambda i, c: (attend(me, mate, i), c)[1], 0)

    for step in range(1, rows):
        origin = row_source(step) * 2
        near, far = origin + core, origin + 1 - core

        def arriving(i, carry, step=step, near=near, far=far):
            place = pl.ds(pl.multiple_of(i * BLOCK, BLOCK), BLOCK)
            remote(
                k_ref.at[place], k_all.at[near, place],
                row_send.at[step - 1, 0, i], row_recv.at[step - 1, 0, i], mate_id,
            ).wait_recv()
            remote(
                k_all.at[near, place], k_all.at[near, place],
                pass_send.at[step - 1, 0, i], pass_recv.at[step - 1, 0, i], mate_id,
            ).start()
            remote(
                v_all.at[near, i], v_all.at[near, i],
                row_send.at[step - 1, 1, i], row_recv.at[step - 1, 1, i], mate_id,
            ).wait_recv()
            remote(
                v_all.at[near, i], v_all.at[near, i],
                pass_send.at[step - 1, 1, i], pass_recv.at[step - 1, 1, i], mate_id,
            ).start()
            remote(
                k_all.at[far, place], k_all.at[far, place],
                pass_send.at[step - 1, 0, i], pass_recv.at[step - 1, 0, i], mate_id,
            ).wait_recv()
            remote(
                v_all.at[far, i], v_all.at[far, i],
                pass_send.at[step - 1, 1, i], pass_recv.at[step - 1, 1, i], mate_id,
            ).wait_recv()
            attend(near, far, i)
            return carry

        lax.fori_loop(0, blocks, arriving, 0)

    for b in range(blocks):
        for g in range(groups):
            parts = []
            for j in range(per_group):
                at = g * GROUP + j * head_dim
                cols = slice(j * BLOCK, (j + 1) * BLOCK)
                parts.append(accum[b, at : at + head_dim] / total[b, g : g + 1, cols])
            mixed_ref[b * BLOCK : (b + 1) * BLOCK, g * GROUP : (g + 1) * GROUP] = (
                jnp.concatenate(parts, axis=0).T.astype(BF16)
            )

    key_mate.wait_send()
    value_mate.wait_send()
    for step in range(1, rows):
        near = row_source(step) * 2 + core
        for i in range(blocks):
            place = slice(i * BLOCK, (i + 1) * BLOCK)
            key_row_copy(step, i).wait_send()
            value_row_copy(step, i).wait_send()
            remote(
                k_all.at[near, place], k_all.at[near, place],
                pass_send.at[step - 1, 0, i], pass_recv.at[step - 1, 0, i], mate_id,
            ).wait_send()
            remote(
                v_all.at[near, i], v_all.at[near, i],
                pass_send.at[step - 1, 1, i], pass_recv.at[step - 1, 1, i], mate_id,
            ).wait_send()


def attention(pattern, queries, keys, values, n_seq):
    points, width = queries.shape
    head_dim = width // HEADS
    blocks = points // BLOCK
    groups = width // GROUP
    rows = n_seq // 2
    wide = GROUP // head_dim * BLOCK
    vmem = pl.BlockSpec(memory_space=pltpu.VMEM)
    hops = max(rows - 1, 1)
    return pl.pallas_call(
        functools.partial(attention_kernel, n_seq, head_dim),
        out_shape=jax.ShapeDtypeStruct((points, width), BF16),
        in_specs=[pl.BlockSpec(memory_space=pltpu.SMEM)] + [pl.BlockSpec(memory_space=pltpu.HBM)] * 3,
        out_specs=vmem,
        scratch_shapes=[
            pltpu.VMEM((points, width), BF16),
            pltpu.VMEM((points, width), BF16),
            pltpu.VMEM((n_seq, points, width), BF16),
            pltpu.VMEM((n_seq, blocks, width, BLOCK), BF16),
            pltpu.VMEM((blocks, groups, 2 * GROUP, wide), BF16),
            pltpu.VMEM((blocks, groups, wide), F32),
            pltpu.VMEM((blocks, groups, wide), F32),
            pltpu.VMEM((blocks, width, BLOCK), F32),
            pltpu.SemaphoreType.DMA((3,)),
            pltpu.SemaphoreType.DMA((2,)),
            pltpu.SemaphoreType.DMA((2,)),
            pltpu.SemaphoreType.DMA((hops, 2, blocks)),
            pltpu.SemaphoreType.DMA((hops, 2, blocks)),
            pltpu.SemaphoreType.DMA((hops, 2, blocks)),
            pltpu.SemaphoreType.DMA((hops, 2, blocks)),
        ],
        compiler_params=pltpu.CompilerParams(
            collective_id=0, has_side_effects=True, vmem_limit_bytes=63 * 1024 * 1024
        ),
    )(pattern, queries, keys, values)


def contrast_kernel(
    n_seq, n_plane, n_event,
    mixed_ref, weight_ref, served_ref, rows_ref, slot_ref, live_ref,
    grad_ref, loss_ref,
    outgoing, contenders, direction, inverse, units, turned, logits, slopes, embed_grads,
    part_out, part_in, event_all, plane_stat, event_stat,
    go_send, go_recv, part_send, part_recv,
    event_send, event_recv, whole_send, whole_recv,
    pstat_send, pstat_recv, estat_send, estat_recv,
):
    points, width = mixed_ref.shape
    capacity = served_ref.shape[1]
    anchors_dev = rows_ref.shape[1]
    chunk = part_out.shape[2]
    cands = n_plane * capacity
    n_view, n_row = n_plane // n_seq, n_seq // 2
    my_view, my_seq = lax.axis_index("view"), lax.axis_index("seq")
    my_row, my_core = my_seq // 2, my_seq % 2
    me = my_view * n_seq + my_seq
    my_event = lax.axis_index("event")

    def seat(step, way):
        view = lax.rem(my_view + n_view + way * step[0], n_view)
        row = lax.rem(my_row + n_row + way * step[1], n_row)
        core = lax.rem(my_core + 2 + way * step[2], 2)
        return view, row * 2 + core

    def target(step):
        view, seq = seat(step, 1)
        return view * n_seq + seq, {"view": view, "seq": seq}

    def source(step):
        view, seq = seat(step, -1)
        return view * n_seq + seq

    def event_at(step):
        return lax.rem(my_event + step, n_event)

    steps = [
        (a, b, c) for a in range(n_view) for b in range(n_row) for c in range(2) if a or b or c
    ]
    steps.sort(key=lambda s: (-(s[0] > 0) - (s[1] > 0), s[2], s[0]))
    greet(
        [target(step)[1] for step in steps]
        + [{"event": event_at(step)} for step in range(1, n_event)]
    )

    def push(src, dst, send, recv, step):
        peer, device = target(step)
        return remote(src, dst.at[me], send.at[peer], recv.at[me], device)

    def pull(dst, send, recv, step):
        peer = source(step)
        return remote(dst.at[peer], dst.at[peer], send.at[peer], recv.at[peer], target(step)[1])

    point_index = lax.broadcasted_iota(jnp.int32, (points, capacity), 0)

    def gather(peer):
        pick = jnp.where(served_ref[pl.ds(peer, 1), :] == point_index, 1.0, 0.0).astype(BF16)
        return jnp.dot(pick.T, mixed_ref[...], preferred_element_type=F32).astype(BF16)

    for step in steps:
        peer = target(step)[0]
        outgoing[peer] = gather(peer)
        push(outgoing.at[peer], contenders, go_send, go_recv, step).start()
    contenders[me] = gather(me)

    anchor_pick = jnp.where(
        rows_ref[...] == lax.broadcasted_iota(jnp.int32, (points, anchors_dev), 0), 1.0, 0.0
    ).astype(BF16)
    anchor_mixed = jnp.dot(anchor_pick.T, mixed_ref[...], preferred_element_type=F32).astype(BF16)

    def project(rows_mixed, at):
        place = slice(at, at + rows_mixed.shape[0])
        embed = jnp.dot(rows_mixed, weight_ref[...], preferred_element_type=F32)
        scale = lax.rsqrt(jnp.sum(embed * embed, axis=-1, keepdims=True) + 1e-06)
        embed = embed * scale
        inverse[place] = scale
        direction[place] = embed
        units[place] = embed.astype(BF16)
        turned[:, place] = rows_mixed.T

    project(anchor_mixed, cands)
    anchors = units[cands:]
    live = live_ref[...].astype(F32)
    slots = slot_ref[...]
    slot_index = lax.broadcasted_iota(jnp.int32, (capacity, anchors_dev), 0)

    def correct(peer):
        return jnp.where(slots - peer * capacity == slot_index, 1.0, 0.0)

    sums = jnp.zeros((1, anchors_dev), F32)
    goal = jnp.zeros((1, anchors_dev), F32)
    arrivals = [None] + steps[-1:] + steps[:-1]
    origins = [source(step) if step else me for step in arrivals]
    for at, step in enumerate(arrivals):
        peer = origins[at]
        if step:
            pull(contenders, go_send, go_recv, step).wait_recv()
        place = slice(at * capacity, (at + 1) * capacity)
        project(contenders[peer], at * capacity)
        scores = lax.dot_general(
            units[place], anchors, (((1,), (1,)), ((), ())), preferred_element_type=F32
        ) / SHARPNESS_SCALE
        grown = jnp.exp(scores)
        logits[place] = grown
        sums = sums + jnp.sum(grown, axis=0, keepdims=True)
        goal = goal + jnp.sum(scores * correct(peer), axis=0, keepdims=True)
    loss_part = jnp.sum(live * (jnp.log(sums) - goal), axis=1, keepdims=True)
    live_part = jnp.sum(live, axis=1, keepdims=True)
    row_index = lax.broadcasted_iota(jnp.int32, (8, 128), 0)
    plane_stat[me] = jnp.where(row_index == 0, loss_part, live_part)
    for step in steps:
        push(plane_stat.at[me], plane_stat, pstat_send, pstat_recv, step).start()

    for at, peer in enumerate(origins):
        place = slice(at * capacity, (at + 1) * capacity)
        slopes[place] = (
            live * (logits[place] / sums - correct(peer)) / SHARPNESS_SCALE
        ).astype(BF16)

    def pull_back(grads, place):
        along = direction[place]
        inner = jnp.sum(along * grads, axis=-1, keepdims=True)
        embed_grads[place] = (inverse[place] * (grads - along * inner)).astype(BF16)

    for at in range(0, cands, anchors_dev):
        place = slice(at, at + anchors_dev)
        pull_back(jnp.dot(slopes[place], anchors, preferred_element_type=F32), place)
    pull_back(
        jnp.dot(slopes[...].T, units[:cands], preferred_element_type=F32),
        slice(cands, cands + anchors_dev),
    )
    parts = [slice(at, at + GROUP) for at in range(0, width, GROUP)]
    for n, cols in enumerate(parts):
        part = jnp.dot(turned[...], embed_grads[:, cols], preferred_element_type=F32)
        part_out[n] = part.astype(BF16).reshape(n_plane, chunk, GROUP)
        for step in steps:
            peer = target(step)[0]
            push(
                part_out.at[n, peer], part_in.at[n], part_send.at[n], part_recv.at[n], step
            ).start()
        part_in[n, me] = part_out[n, me]

    for step in steps:
        pull(plane_stat, pstat_send, pstat_recv, step).wait_recv()
    stat = plane_stat[0]
    for p in range(1, n_plane):
        stat = stat + plane_stat[p]
    event_stat[my_event] = stat

    def event_swap(array, send, recv, step, slot):
        event = event_at(step)
        return remote(
            array.at[my_event], array.at[slot], send.at[event], recv.at[slot], {"event": event}
        )

    for step in range(1, n_event):
        event_swap(event_stat, estat_send, estat_recv, step, my_event).start()

    for n in range(len(parts)):
        for step in steps:
            pull(part_in.at[n], part_send.at[n], part_recv.at[n], step).wait_recv()
        reduced = part_in[n, 0].astype(F32)
        for p in range(1, n_plane):
            reduced = reduced + part_in[n, p].astype(F32)
        event_all[n, my_event] = reduced.astype(BF16)
        for step in range(1, n_event):
            event_swap(
                event_all.at[n], event_send.at[n], event_recv.at[n], step, my_event
            ).start()

    def spread(n, cols, step):
        peer, device = target(step)
        mine = grad_ref.at[me, :, cols]
        return remote(mine, mine, whole_send.at[n, peer], whole_recv.at[n, me], device)

    def landed(n, cols, step):
        peer = source(step)
        theirs = grad_ref.at[peer, :, cols]
        return remote(
            theirs, theirs, whole_send.at[n, peer], whole_recv.at[n, peer], target(step)[1]
        )

    for n, cols in enumerate(parts):
        for step in range(1, n_event):
            event_swap(
                event_all.at[n], event_send.at[n], event_recv.at[n], step, event_at(step)
            ).wait_recv()
        reduced = event_all[n, 0].astype(F32)
        for e in range(1, n_event):
            reduced = reduced + event_all[n, e].astype(F32)
        grad_ref[me, :, cols] = reduced.astype(BF16)
        for step in steps:
            spread(n, cols, step).start()

    for step in range(1, n_event):
        event_swap(event_stat, estat_send, estat_recv, step, event_at(step)).wait_recv()
    stat = event_stat[0]
    for e in range(1, n_event):
        stat = stat + event_stat[e]
    loss_ref[0, 0] = jnp.max(stat[0:1] / stat[1:2])

    for step in steps:
        peer = target(step)[0]
        push(outgoing.at[peer], contenders, go_send, go_recv, step).wait_send()
        push(plane_stat.at[me], plane_stat, pstat_send, pstat_recv, step).wait_send()
        for n, cols in enumerate(parts):
            push(
                part_out.at[n, peer], part_in.at[n], part_send.at[n], part_recv.at[n], step
            ).wait_send()
    for step in range(1, n_event):
        event_swap(event_stat, estat_send, estat_recv, step, my_event).wait_send()
        for n in range(len(parts)):
            event_swap(
                event_all.at[n], event_send.at[n], event_recv.at[n], step, my_event
            ).wait_send()
    for n, cols in enumerate(parts):
        for step in steps:
            landed(n, cols, step).wait_recv()
    for n, cols in enumerate(parts):
        for step in steps:
            spread(n, cols, step).wait_send()


def contrast(mixed, out_weight, served, rows, slots, live, n_seq, n_plane, n_event):
    points, width = mixed.shape
    senders, capacity = served.shape
    anchors_dev = rows.shape[1]
    chunk = width // n_plane
    cands = senders * capacity
    every = cands + anchors_dev
    vmem = pl.BlockSpec(memory_space=pltpu.VMEM)
    parts = width // GROUP

    def sems(*dims):
        return [pltpu.SemaphoreType.DMA(dims)] * 2

    return pl.pallas_call(
        functools.partial(contrast_kernel, n_seq, n_plane, n_event),
        out_shape=(
            jax.ShapeDtypeStruct((n_plane, chunk, width), BF16),
            jax.ShapeDtypeStruct((1, 1), F32),
        ),
        in_specs=[vmem] * 6,
        out_specs=(vmem, pl.BlockSpec(memory_space=pltpu.SMEM)),
        scratch_shapes=[
            pltpu.VMEM((senders, capacity, width), BF16),
            pltpu.VMEM((senders, capacity, width), BF16),
            pltpu.VMEM((every, width), F32),
            pltpu.VMEM((every, 1), F32),
            pltpu.VMEM((every, width), BF16),
            pltpu.VMEM((width, every), BF16),
            pltpu.VMEM((cands, anchors_dev), F32),
            pltpu.VMEM((cands, anchors_dev), BF16),
            pltpu.VMEM((every, width), BF16),
            pltpu.VMEM((parts, n_plane, chunk, GROUP), BF16),
            pltpu.VMEM((parts, n_plane, chunk, GROUP), BF16),
            pltpu.VMEM((parts, n_event, chunk, GROUP), BF16),
            pltpu.VMEM((n_plane, 8, 128), F32),
            pltpu.VMEM((n_event, 8, 128), F32),
        ]
        + sems(n_plane)
        + sems(parts, n_plane)
        + sems(parts, n_event)
        + sems(parts, n_plane)
        + sems(n_plane)
        + sems(n_event),
        compiler_params=pltpu.CompilerParams(
            collective_id=1, has_side_effects=True, vmem_limit_bytes=40 * 1024 * 1024
        ),
    )(mixed, out_weight, served, rows, slots, live)


def per_device(
    query, key, value, pattern, out_weight, served, anchor_rows, positive_slot, anchor_live
):
    n_view, n_seq, n_event = (lax.axis_size(name) for name in ("view", "seq", "event"))
    mixed = attention(pattern[0].transpose(1, 0, 2), query[0, 0], key[0, 0], value[0, 0], n_seq)
    grad, loss = contrast(
        mixed, out_weight, served[0, 0], anchor_rows[0], positive_slot[0], anchor_live[0],
        n_seq, n_view * n_seq, n_event,
    )
    grad = grad.reshape(out_weight.shape).astype(F32)
    return (mixed[None, None], grad, loss[0, 0])


def solution(mesh):
    placed = (
        P("event", "view", "seq", None),
        P("event", "view", "seq", None),
        P("event", "view", "seq", None),
        P("event", "view", "seq", None),
        P(),
        P("event", "view", "seq", None),
        P("event", "view", "seq"),
        P("event", "view", "seq"),
        P("event", "view", "seq"),
    )
    return jax.shard_map(
        per_device,
        mesh=mesh,
        in_specs=placed,
        out_specs=(P("event", "view", "seq", None), P(), P()),
        check_vma=False,
    )
```

```python
import functools
import math

import jax
import jax.numpy as jnp
from jax import lax
from jax.experimental import pallas as pl
from jax.experimental.pallas import tpu as pltpu
from jax.sharding import PartitionSpec as P

HEADS = 16
BLOCK = 128
GROUP = 128
NEGATIVE = -1e30
SHARPNESS_SCALE = 0.07
F32 = jnp.float32
BF16 = jnp.bfloat16


def remote(src, dst, send, recv, device):
    return pltpu.make_async_remote_copy(
        src_ref=src,
        dst_ref=dst,
        send_sem=send,
        recv_sem=recv,
        device_id=device,
        device_id_type=pl.DeviceIdType.MESH,
    )


def greet(devices):
    barrier = pltpu.get_barrier_semaphore()
    for device in devices:
        pl.semaphore_signal(
            barrier, inc=1, device_id=device, device_id_type=pl.DeviceIdType.MESH
        )
    pl.semaphore_wait(barrier, len(devices))


def seats(n_seq, n_plane, n_event):
    n_view, n_row = n_plane // n_seq, n_seq // 2
    my_view, my_seq = lax.axis_index("view"), lax.axis_index("seq")
    my_row, my_core = my_seq // 2, my_seq % 2
    me = my_view * n_seq + my_seq
    my_event = lax.axis_index("event")

    def seat(step, way):
        view = lax.rem(my_view + n_view + way * step[0], n_view)
        row = lax.rem(my_row + n_row + way * step[1], n_row)
        core = lax.rem(my_core + 2 + way * step[2], 2)
        return view, row * 2 + core

    def target(step):
        view, seq = seat(step, 1)
        return view * n_seq + seq, {"view": view, "seq": seq}

    def source(step):
        view, seq = seat(step, -1)
        return view * n_seq + seq

    def event_at(step):
        return lax.rem(my_event + step, n_event)

    steps = [
        (a, b, c) for a in range(n_view) for b in range(n_row) for c in range(2) if a or b or c
    ]
    steps.sort(key=lambda s: (-(s[0] > 0) - (s[1] > 0), s[2], s[0]))
    return my_event, me, target, source, event_at, steps


def attend_part(
    n_seq, head_dim, arrive, pattern, q_ref, k_ref, v_ref, mixed_ref,
    q_in, v_in, k_all, v_all, q_wide, best, total, accum, load_sem,
    mate_send, mate_recv, row_send, row_recv, pass_send, pass_recv,
):
    points, width = q_ref.shape
    blocks = points // BLOCK
    groups = width // GROUP
    per_group = GROUP // head_dim
    rows = n_seq // 2
    me = lax.axis_index("seq")
    my_row, core = me // 2, me % 2
    mate = my_row * 2 + 1 - core
    mate_id = {"seq": mate}

    def row_peer(step):
        return lax.rem(my_row + step, rows) * 2 + core

    def row_source(step):
        return lax.rem(my_row + rows - step, rows)

    loads = [
        pltpu.make_async_copy(src, dst, load_sem.at[n])
        for n, (src, dst) in enumerate(((v_ref, v_in), (q_ref, q_in), (k_ref, k_all.at[me])))
    ]
    for load in loads:
        load.start()
    arrive()

    def key_row_copy(step, i):
        place = pl.ds(pl.multiple_of(i * BLOCK, BLOCK), BLOCK)
        return remote(
            k_ref.at[place], k_all.at[me, place],
            row_send.at[step - 1, 0, i], row_recv.at[step - 1, 0, i],
            {"seq": row_peer(step)},
        )

    def value_row_copy(step, i):
        return remote(
            v_all.at[me, i], v_all.at[me, i],
            row_send.at[step - 1, 1, i], row_recv.at[step - 1, 1, i],
            {"seq": row_peer(step)},
        )

    key_mate = remote(k_ref, k_all.at[me], mate_send.at[0], mate_recv.at[0], mate_id)
    value_mate = remote(
        v_all.at[me], v_all.at[me], mate_send.at[1], mate_recv.at[1], mate_id
    )

    key_row_copy(1, 0).start()
    loads[0].wait()
    for i in range(blocks):
        v_all[me, i] = v_in[i * BLOCK : (i + 1) * BLOCK, :].T
        for step in range(1, rows):
            if step > 1 or i > 0:
                key_row_copy(step, i).start()
            value_row_copy(step, i).start()
    key_mate.start()
    value_mate.start()
    loads[1].wait()
    factor_in = head_dim ** (-0.5) * math.log2(math.e)
    q_wide[...] = jnp.zeros_like(q_wide)
    for b in range(blocks):
        turned = q_in[b * BLOCK : (b + 1) * BLOCK, :].T.astype(F32) * factor_in
        high = turned.astype(BF16)
        low = (turned - high.astype(F32)).astype(BF16)
        for g in range(groups):
            for j in range(per_group):
                at = g * GROUP + j * head_dim
                cols = slice(j * BLOCK, (j + 1) * BLOCK)
                q_wide[b, g, j * head_dim : (j + 1) * head_dim, cols] = high[at : at + head_dim]
                q_wide[b, g, GROUP + j * head_dim : GROUP + (j + 1) * head_dim, cols] = low[
                    at : at + head_dim
                ]
    best[...] = jnp.full_like(best, NEGATIVE)
    total[...] = jnp.zeros_like(total)
    accum[...] = jnp.zeros_like(accum)

    ones = jnp.ones((16, BLOCK), BF16)

    def attend(first, second, i):
        place = pl.ds(pl.multiple_of(i * BLOCK, BLOCK), BLOCK)
        sources = (first, second)
        keeps = [
            [pattern[b, 0, source * blocks + i].astype(F32) for source in sources]
            for b in range(blocks)
        ]

        def scores_of(b, g):
            lanes = slice(g * GROUP, (g + 1) * GROUP)
            keys = jnp.concatenate([k_all[source, place, lanes] for source in sources], axis=0)
            return jnp.dot(
                jnp.concatenate([keys, keys], axis=1), q_wide[b, g], preferred_element_type=F32
            )

        def finish(b, g, scores):
            lanes = slice(g * GROUP, (g + 1) * GROUP)
            halves = [scores[:BLOCK], scores[BLOCK:]]
            tops = [jnp.max(half, axis=0, keepdims=True) for half in halves]
            old = best[b, g : g + 1]
            new = old
            for top, keep in zip(tops, keeps[b]):
                new = jnp.maximum(new, top + (keep - 1.0) * (-NEGATIVE))
            weights = jnp.concatenate(
                [
                    jnp.exp2(half - jnp.maximum(new, top)).astype(BF16)
                    for half, top in zip(halves, tops)
                ],
                axis=0,
            )
            fade = jnp.exp2(old - new)
            best[b, g : g + 1] = new
            vals = [
                jnp.concatenate([v_all[source, i, lanes, :], ones], axis=0) * keep.astype(BF16)
                for source, keep in zip(sources, keeps[b])
            ]
            vals = jnp.concatenate(vals, axis=1)
            pair = 2 * head_dim
            for n in range(per_group // 2):
                cols = slice(2 * n * BLOCK, (2 * n + 2) * BLOCK)
                rows_in = jnp.concatenate([vals[n * pair : (n + 1) * pair], vals[GROUP:]], axis=0)
                out = jnp.dot(rows_in, weights[:, cols], preferred_element_type=F32)
                total[b, g : g + 1, cols] = (
                    total[b, g : g + 1, cols] * fade[:, cols] + out[pair : pair + 1]
                )
                for j in range(2):
                    at = g * GROUP + (2 * n + j) * head_dim
                    side = slice(j * BLOCK, (j + 1) * BLOCK)
                    accum[b, at : at + head_dim] = (
                        accum[b, at : at + head_dim] * fade[:, cols][:, side]
                        + out[j * head_dim : (j + 1) * head_dim, side]
                    )

        units = [(b, g) for b in range(blocks) for g in range(groups)]
        ready = scores_of(*units[0])
        for at, unit in enumerate(units):
            later = scores_of(*units[at + 1]) if at + 1 < len(units) else None
            finish(*unit, ready)
            ready = later

    loads[2].wait()
    remote(k_ref, k_all.at[mate], mate_send.at[0], mate_recv.at[0], mate_id).wait_recv()
    remote(
        v_all.at[mate], v_all.at[mate], mate_send.at[1], mate_recv.at[1], mate_id
    ).wait_recv()
    lax.fori_loop(0, blocks, lambda i, c: (attend(me, mate, i), c)[1], 0)

    for step in range(1, rows):
        origin = row_source(step) * 2
        near, far = origin + core, origin + 1 - core

        def arriving(i, carry, step=step, near=near, far=far):
            place = pl.ds(pl.multiple_of(i * BLOCK, BLOCK), BLOCK)
            remote(
                k_ref.at[place], k_all.at[near, place],
                row_send.at[step - 1, 0, i], row_recv.at[step - 1, 0, i], mate_id,
            ).wait_recv()
            remote(
                k_all.at[near, place], k_all.at[near, place],
                pass_send.at[step - 1, 0, i], pass_recv.at[step - 1, 0, i], mate_id,
            ).start()
            remote(
                v_all.at[near, i], v_all.at[near, i],
                row_send.at[step - 1, 1, i], row_recv.at[step - 1, 1, i], mate_id,
            ).wait_recv()
            remote(
                v_all.at[near, i], v_all.at[near, i],
                pass_send.at[step - 1, 1, i], pass_recv.at[step - 1, 1, i], mate_id,
            ).start()
            remote(
                k_all.at[far, place], k_all.at[far, place],
                pass_send.at[step - 1, 0, i], pass_recv.at[step - 1, 0, i], mate_id,
            ).wait_recv()
            remote(
                v_all.at[far, i], v_all.at[far, i],
                pass_send.at[step - 1, 1, i], pass_recv.at[step - 1, 1, i], mate_id,
            ).wait_recv()
            attend(near, far, i)
            return carry

        lax.fori_loop(0, blocks, arriving, 0)

    for b in range(blocks):
        for g in range(groups):
            parts = []
            share = 1.0 / total[b, g : g + 1]
            for j in range(per_group):
                at = g * GROUP + j * head_dim
                cols = slice(j * BLOCK, (j + 1) * BLOCK)
                parts.append(accum[b, at : at + head_dim] * share[:, cols])
            mixed_ref[b * BLOCK : (b + 1) * BLOCK, g * GROUP : (g + 1) * GROUP] = (
                jnp.concatenate(parts, axis=0).T.astype(BF16)
            )

    key_mate.wait_send()
    value_mate.wait_send()
    for step in range(1, rows):
        near = row_source(step) * 2 + core
        for i in range(blocks):
            place = slice(i * BLOCK, (i + 1) * BLOCK)
            key_row_copy(step, i).wait_send()
            value_row_copy(step, i).wait_send()
            remote(
                k_all.at[near, place], k_all.at[near, place],
                pass_send.at[step - 1, 0, i], pass_recv.at[step - 1, 0, i], mate_id,
            ).wait_send()
            remote(
                v_all.at[near, i], v_all.at[near, i],
                pass_send.at[step - 1, 1, i], pass_recv.at[step - 1, 1, i], mate_id,
            ).wait_send()


def contrast_part(
    n_seq, n_plane, n_event, early, mixed_ref, weight_ref, served_ref, rows_ref, slot_ref, live_ref,
    grad_ref, loss_ref,
    outgoing, contenders, direction, inverse, units, turned, logits, slopes, embed_grads,
    part_out, part_in, event_all, plane_stat, event_stat,
    go_send, go_recv, part_send, part_recv,
    event_send, event_recv, whole_send, whole_recv,
    pstat_send, pstat_recv, estat_send, estat_recv,
):
    points, width = mixed_ref.shape
    capacity = served_ref.shape[1]
    anchors_dev = rows_ref.shape[1]
    chunk = part_out.shape[2]
    cands = n_plane * capacity
    my_event, me, target, source, event_at, steps = early

    def push(src, dst, send, recv, step):
        peer, device = target(step)
        return remote(src, dst.at[me], send.at[peer], recv.at[me], device)

    def pull(dst, send, recv, step):
        peer = source(step)
        return remote(dst.at[peer], dst.at[peer], send.at[peer], recv.at[peer], target(step)[1])

    point_index = lax.broadcasted_iota(jnp.int32, (points, capacity), 0)

    def gather(peer):
        pick = jnp.where(served_ref[pl.ds(peer, 1), :] == point_index, 1.0, 0.0).astype(BF16)
        return jnp.dot(pick.T, mixed_ref[...], preferred_element_type=F32).astype(BF16)

    for step in steps:
        peer = target(step)[0]
        outgoing[peer] = gather(peer)
        push(outgoing.at[peer], contenders, go_send, go_recv, step).start()
    contenders[me] = gather(me)

    anchor_pick = jnp.where(
        rows_ref[...] == lax.broadcasted_iota(jnp.int32, (points, anchors_dev), 0), 1.0, 0.0
    ).astype(BF16)
    anchor_mixed = jnp.dot(anchor_pick.T, mixed_ref[...], preferred_element_type=F32).astype(BF16)

    def project(rows_mixed, at):
        place = slice(at, at + rows_mixed.shape[0])
        embed = jnp.dot(rows_mixed, weight_ref[...], preferred_element_type=F32)
        scale = lax.rsqrt(jnp.sum(embed * embed, axis=-1, keepdims=True) + 1e-06)
        embed = embed * scale
        inverse[place] = scale
        direction[place] = embed
        units[place] = embed.astype(BF16)
        turned[:, place] = rows_mixed.T

    project(anchor_mixed, cands)
    anchors = units[cands:]
    anchors_turned = anchors.T
    live = live_ref[...].astype(F32)
    slots = slot_ref[...]
    slot_index = lax.broadcasted_iota(jnp.int32, (capacity, anchors_dev), 0)

    def correct(peer):
        return jnp.where(slots - peer * capacity == slot_index, 1.0, 0.0)

    sums = jnp.zeros((1, anchors_dev), F32)
    goal = jnp.zeros((1, anchors_dev), F32)
    arrivals = [None] + steps[-1:] + steps[:-1]
    origins = [source(step) if step else me for step in arrivals]
    for at, step in enumerate(arrivals):
        peer = origins[at]
        if step:
            pull(contenders, go_send, go_recv, step).wait_recv()
        place = slice(at * capacity, (at + 1) * capacity)
        project(contenders[peer], at * capacity)
        scores = jnp.dot(units[place], anchors_turned, preferred_element_type=F32)
        scores = scores * (1.0 / SHARPNESS_SCALE)
        grown = jnp.exp(scores)
        logits[place] = grown
        sums = sums + jnp.sum(grown, axis=0, keepdims=True)
        goal = goal + jnp.sum(scores * correct(peer), axis=0, keepdims=True)
    loss_part = jnp.sum(live * (jnp.log(sums) - goal), axis=1, keepdims=True)
    live_part = jnp.sum(live, axis=1, keepdims=True)
    row_index = lax.broadcasted_iota(jnp.int32, (8, 128), 0)
    plane_stat[me] = jnp.where(row_index == 0, loss_part, live_part)
    for step in steps:
        push(plane_stat.at[me], plane_stat, pstat_send, pstat_recv, step).start()

    pull_up = live * (1.0 / SHARPNESS_SCALE)
    share = pull_up / sums
    for at, peer in enumerate(origins):
        place = slice(at * capacity, (at + 1) * capacity)
        slopes[place] = (logits[place] * share - correct(peer) * pull_up).astype(BF16)

    def pull_back(grads, place):
        along = direction[place]
        inner = jnp.sum(along * grads, axis=-1, keepdims=True)
        embed_grads[place] = (inverse[place] * (grads - along * inner)).astype(BF16)

    for at in range(0, cands, anchors_dev):
        place = slice(at, at + anchors_dev)
        pull_back(jnp.dot(slopes[place], anchors, preferred_element_type=F32), place)
    pull_back(
        jnp.dot(slopes[...].T, units[:cands], preferred_element_type=F32),
        slice(cands, cands + anchors_dev),
    )
    parts = [slice(at, at + GROUP) for at in range(0, width, GROUP)]
    for n, cols in enumerate(parts):
        part = jnp.dot(turned[...], embed_grads[:, cols], preferred_element_type=F32)
        part_out[n] = part.astype(BF16).reshape(n_plane, chunk, GROUP)
        for step in steps:
            peer = target(step)[0]
            push(
                part_out.at[n, peer], part_in.at[n], part_send.at[n], part_recv.at[n], step
            ).start()
        part_in[n, me] = part_out[n, me]

    for step in steps:
        pull(plane_stat, pstat_send, pstat_recv, step).wait_recv()
    stat = plane_stat[0]
    for p in range(1, n_plane):
        stat = stat + plane_stat[p]
    event_stat[my_event] = stat

    def event_swap(array, send, recv, step, slot):
        event = event_at(step)
        return remote(
            array.at[my_event], array.at[slot], send.at[event], recv.at[slot], {"event": event}
        )

    for step in range(1, n_event):
        event_swap(event_stat, estat_send, estat_recv, step, my_event).start()

    for n in range(len(parts)):
        for step in steps:
            pull(part_in.at[n], part_send.at[n], part_recv.at[n], step).wait_recv()
        reduced = part_in[n, 0].astype(F32)
        for p in range(1, n_plane):
            reduced = reduced + part_in[n, p].astype(F32)
        event_all[n, my_event] = reduced.astype(BF16)
        for step in range(1, n_event):
            event_swap(
                event_all.at[n], event_send.at[n], event_recv.at[n], step, my_event
            ).start()

    def spread(n, cols, step):
        peer, device = target(step)
        mine = grad_ref.at[me, :, cols]
        return remote(mine, mine, whole_send.at[n, peer], whole_recv.at[n, me], device)

    def landed(n, cols, step):
        peer = source(step)
        theirs = grad_ref.at[peer, :, cols]
        return remote(
            theirs, theirs, whole_send.at[n, peer], whole_recv.at[n, peer], target(step)[1]
        )

    for n, cols in enumerate(parts):
        for step in range(1, n_event):
            event_swap(
                event_all.at[n], event_send.at[n], event_recv.at[n], step, event_at(step)
            ).wait_recv()
        reduced = event_all[n, 0].astype(F32)
        for e in range(1, n_event):
            reduced = reduced + event_all[n, e].astype(F32)
        grad_ref[me, :, cols] = reduced.astype(BF16)
        for step in steps:
            spread(n, cols, step).start()

    for step in range(1, n_event):
        event_swap(event_stat, estat_send, estat_recv, step, event_at(step)).wait_recv()
    stat = event_stat[0]
    for e in range(1, n_event):
        stat = stat + event_stat[e]
    loss_ref[0, 0] = jnp.max(stat[0:1] / stat[1:2])

    for step in steps:
        peer = target(step)[0]
        push(outgoing.at[peer], contenders, go_send, go_recv, step).wait_send()
        push(plane_stat.at[me], plane_stat, pstat_send, pstat_recv, step).wait_send()
        for n, cols in enumerate(parts):
            push(
                part_out.at[n, peer], part_in.at[n], part_send.at[n], part_recv.at[n], step
            ).wait_send()
    for step in range(1, n_event):
        event_swap(event_stat, estat_send, estat_recv, step, my_event).wait_send()
        for n in range(len(parts)):
            event_swap(
                event_all.at[n], event_send.at[n], event_recv.at[n], step, my_event
            ).wait_send()
    for n, cols in enumerate(parts):
        for step in steps:
            landed(n, cols, step).wait_recv()
    for n, cols in enumerate(parts):
        for step in steps:
            spread(n, cols, step).wait_send()


def whole_kernel(
    n_seq, n_plane, n_event, head_dim, n_attend,
    pattern, q_ref, k_ref, v_ref, weight_hbm, served_hbm, rows_hbm, slot_hbm, live_hbm,
    mixed_ref, grad_ref, loss_ref,
    weight_ref, served_ref, rows_ref, slot_ref, live_ref, input_sem, *scratch,
):
    early = seats(n_seq, n_plane, n_event)
    my_event, me, target, source, event_at, steps = early
    pairs = (
        (weight_hbm, weight_ref), (served_hbm, served_ref), (rows_hbm, rows_ref),
        (slot_hbm, slot_ref), (live_hbm, live_ref),
    )
    inputs = [
        pltpu.make_async_copy(src, dst, input_sem.at[n]) for n, (src, dst) in enumerate(pairs)
    ]

    def arrive():
        for load in inputs:
            load.start()
        greet(
            [target(step)[1] for step in steps]
            + [{"event": event_at(step)} for step in range(1, n_event)]
        )

    attend_part(
        n_seq, head_dim, arrive, pattern, q_ref, k_ref, v_ref, mixed_ref, *scratch[:n_attend]
    )
    for load in inputs:
        load.wait()
    contrast_part(
        n_seq, n_plane, n_event, early, mixed_ref, weight_ref, served_ref, rows_ref, slot_ref,
        live_ref, grad_ref, loss_ref, *scratch[n_attend:],
    )


def per_device(
    query, key, value, pattern, out_weight, served, anchor_rows, positive_slot, anchor_live
):
    n_view, n_seq, n_event = (lax.axis_size(name) for name in ("view", "seq", "event"))
    n_plane = n_view * n_seq
    points, width = query.shape[2:]
    senders, capacity = served.shape[2:]
    anchors_dev = anchor_rows.shape[2]
    head_dim = width // HEADS
    blocks = points // BLOCK
    groups = width // GROUP
    wide = GROUP // head_dim * BLOCK
    hops = max(n_seq // 2 - 1, 1)
    chunk = width // n_plane
    cands = senders * capacity
    every = cands + anchors_dev
    parts = width // GROUP
    dma = pltpu.SemaphoreType.DMA

    def sems(*dims):
        return [dma(dims)] * 2

    inputs = [
        pltpu.VMEM((width, width), BF16),
        pltpu.VMEM((senders, capacity), jnp.int32),
        pltpu.VMEM((1, anchors_dev), jnp.int32),
        pltpu.VMEM((1, anchors_dev), jnp.int32),
        pltpu.VMEM((1, anchors_dev), jnp.int32),
        dma((5,)),
    ]
    attend = [
        pltpu.VMEM((points, width), BF16),
        pltpu.VMEM((points, width), BF16),
        pltpu.VMEM((n_seq, points, width), BF16),
        pltpu.VMEM((n_seq, blocks, width, BLOCK), BF16),
        pltpu.VMEM((blocks, groups, 2 * GROUP, wide), BF16),
        pltpu.VMEM((blocks, groups, wide), F32),
        pltpu.VMEM((blocks, groups, wide), F32),
        pltpu.VMEM((blocks, width, BLOCK), F32),
        dma((3,)),
        *sems(2),
        *sems(hops, 2, blocks),
        *sems(hops, 2, blocks),
    ]
    contrast = [
        pltpu.VMEM((senders, capacity, width), BF16),
        pltpu.VMEM((senders, capacity, width), BF16),
        pltpu.VMEM((every, width), F32),
        pltpu.VMEM((every, 1), F32),
        pltpu.VMEM((every, width), BF16),
        pltpu.VMEM((width, every), BF16),
        pltpu.VMEM((cands, anchors_dev), F32),
        pltpu.VMEM((cands, anchors_dev), BF16),
        pltpu.VMEM((every, width), BF16),
        pltpu.VMEM((parts, n_plane, chunk, GROUP), BF16),
        pltpu.VMEM((parts, n_plane, chunk, GROUP), BF16),
        pltpu.VMEM((parts, n_event, chunk, GROUP), BF16),
        pltpu.VMEM((n_plane, 8, 128), F32),
        pltpu.VMEM((n_event, 8, 128), F32),
        *sems(n_plane),
        *sems(parts, n_plane),
        *sems(parts, n_event),
        *sems(parts, n_plane),
        *sems(n_plane),
        *sems(n_event),
    ]
    smem = pl.BlockSpec(memory_space=pltpu.SMEM)
    vmem = pl.BlockSpec(memory_space=pltpu.VMEM)
    mixed, grad, loss = pl.pallas_call(
        functools.partial(whole_kernel, n_seq, n_plane, n_event, head_dim, len(attend)),
        out_shape=(
            jax.ShapeDtypeStruct((points, width), BF16),
            jax.ShapeDtypeStruct((n_plane, chunk, width), BF16),
            jax.ShapeDtypeStruct((1, 1), F32),
        ),
        in_specs=[smem] + [pl.BlockSpec(memory_space=pltpu.HBM)] * 8,
        out_specs=(vmem, vmem, smem),
        scratch_shapes=inputs + attend + contrast,
        compiler_params=pltpu.CompilerParams(
            collective_id=0, has_side_effects=True, vmem_limit_bytes=63 * 1024 * 1024
        ),
    )(
        pattern[0].transpose(1, 0, 2), query[0, 0], key[0, 0], value[0, 0], out_weight,
        served[0, 0], anchor_rows[0], positive_slot[0], anchor_live[0],
    )
    grad = grad.reshape(out_weight.shape).astype(F32)
    return (mixed[None, None], grad, loss[0, 0])


def solution(mesh):
    placed = (
        P("event", "view", "seq", None),
        P("event", "view", "seq", None),
        P("event", "view", "seq", None),
        P("event", "view", "seq", None),
        P(),
        P("event", "view", "seq", None),
        P("event", "view", "seq"),
        P("event", "view", "seq"),
        P("event", "view", "seq"),
    )
    return jax.shard_map(
        per_device,
        mesh=mesh,
        in_specs=placed,
        out_specs=(P("event", "view", "seq", None), P(), P()),
        check_vma=False,
    )
```

```python
import functools
import math

import jax
import jax.numpy as jnp
from jax import lax
from jax.experimental import pallas as pl
from jax.experimental.pallas import tpu as pltpu
from jax.sharding import PartitionSpec as P

HEADS = 16
BLOCK = 128
GROUP = 128
NEGATIVE = -1e30
SHARPNESS_SCALE = 0.07
F32 = jnp.float32
BF16 = jnp.bfloat16


def remote(src, dst, send, recv, device):
    return pltpu.make_async_remote_copy(
        src_ref=src,
        dst_ref=dst,
        send_sem=send,
        recv_sem=recv,
        device_id=device,
        device_id_type=pl.DeviceIdType.MESH,
    )


def greet(devices):
    barrier = pltpu.get_barrier_semaphore()
    for device in devices:
        pl.semaphore_signal(
            barrier, inc=1, device_id=device, device_id_type=pl.DeviceIdType.MESH
        )
    pl.semaphore_wait(barrier, len(devices))


def seats(n_seq, n_plane, n_event):
    n_view, n_row = n_plane // n_seq, n_seq // 2
    my_view, my_seq = lax.axis_index("view"), lax.axis_index("seq")
    my_row, my_core = my_seq // 2, my_seq % 2
    me = my_view * n_seq + my_seq
    my_event = lax.axis_index("event")

    def seat(step, way):
        view = lax.rem(my_view + n_view + way * step[0], n_view)
        row = lax.rem(my_row + n_row + way * step[1], n_row)
        core = lax.rem(my_core + 2 + way * step[2], 2)
        return view, row * 2 + core

    def target(step):
        view, seq = seat(step, 1)
        return view * n_seq + seq, {"view": view, "seq": seq}

    def source(step):
        view, seq = seat(step, -1)
        return view * n_seq + seq

    def event_at(step):
        return lax.rem(my_event + step, n_event)

    steps = [
        (a, b, c) for a in range(n_view) for b in range(n_row) for c in range(2) if a or b or c
    ]
    steps.sort(key=lambda s: (-(s[0] > 0) - (s[1] > 0), s[2], s[0]))
    return my_event, me, target, source, event_at, steps


def attend_part(
    n_seq, head_dim, arrive, pattern, q_ref, k_ref, v_ref, mixed_ref,
    q_in, v_in, k_all, v_all, q_wide, best, total, accum, load_sem,
    mate_send, mate_recv, row_send, row_recv, pass_send, pass_recv,
):
    points, width = q_ref.shape
    blocks = points // BLOCK
    groups = width // GROUP
    per_group = GROUP // head_dim
    rows = n_seq // 2
    me = lax.axis_index("seq")
    my_row, core = me // 2, me % 2
    mate = my_row * 2 + 1 - core
    mate_id = {"seq": mate}

    def row_peer(step):
        return lax.rem(my_row + step, rows) * 2 + core

    def row_source(step):
        return lax.rem(my_row + rows - step, rows)

    loads = [
        pltpu.make_async_copy(src, dst, load_sem.at[n])
        for n, (src, dst) in enumerate(((v_ref, v_in), (q_ref, q_in), (k_ref, k_all.at[me])))
    ]
    for load in loads:
        load.start()
    arrive()

    def key_row_copy(step, i):
        place = pl.ds(pl.multiple_of(i * BLOCK, BLOCK), BLOCK)
        return remote(
            k_ref.at[place], k_all.at[me, place],
            row_send.at[step - 1, 0, i], row_recv.at[step - 1, 0, i],
            {"seq": row_peer(step)},
        )

    def value_row_copy(step, i):
        return remote(
            v_all.at[me, i], v_all.at[me, i],
            row_send.at[step - 1, 1, i], row_recv.at[step - 1, 1, i],
            {"seq": row_peer(step)},
        )

    key_mate = remote(k_ref, k_all.at[me], mate_send.at[0], mate_recv.at[0], mate_id)
    value_mate = remote(
        v_all.at[me], v_all.at[me], mate_send.at[1], mate_recv.at[1], mate_id
    )

    key_row_copy(1, 0).start()
    loads[0].wait()
    for i in range(blocks):
        v_all[me, i] = v_in[i * BLOCK : (i + 1) * BLOCK, :].T
        for step in range(1, rows):
            if step > 1 or i > 0:
                key_row_copy(step, i).start()
            value_row_copy(step, i).start()
    key_mate.start()
    value_mate.start()
    loads[1].wait()
    factor_in = head_dim ** (-0.5) * math.log2(math.e)
    q_wide[...] = jnp.zeros_like(q_wide)
    for b in range(blocks):
        turned = q_in[b * BLOCK : (b + 1) * BLOCK, :].T.astype(F32) * factor_in
        high = turned.astype(BF16)
        low = (turned - high.astype(F32)).astype(BF16)
        for g in range(groups):
            for j in range(per_group):
                at = g * GROUP + j * head_dim
                cols = slice(j * BLOCK, (j + 1) * BLOCK)
                q_wide[b, g, j * head_dim : (j + 1) * head_dim, cols] = high[at : at + head_dim]
                q_wide[b, g, GROUP + j * head_dim : GROUP + (j + 1) * head_dim, cols] = low[
                    at : at + head_dim
                ]
    best[...] = jnp.full_like(best, NEGATIVE)
    total[...] = jnp.zeros_like(total)
    accum[...] = jnp.zeros_like(accum)

    ones = jnp.ones((16, BLOCK), BF16)

    def attend(first, second, i):
        place = pl.ds(pl.multiple_of(i * BLOCK, BLOCK), BLOCK)
        sources = (first, second)
        keeps = [
            [pattern[b, 0, source * blocks + i].astype(F32) for source in sources]
            for b in range(blocks)
        ]

        def scores_of(b, g):
            lanes = slice(g * GROUP, (g + 1) * GROUP)
            keys = jnp.concatenate([k_all[source, place, lanes] for source in sources], axis=0)
            return jnp.dot(
                jnp.concatenate([keys, keys], axis=1), q_wide[b, g], preferred_element_type=F32
            )

        def finish(b, g, scores):
            lanes = slice(g * GROUP, (g + 1) * GROUP)
            halves = [scores[:BLOCK], scores[BLOCK:]]
            tops = [jnp.max(half, axis=0, keepdims=True) for half in halves]
            old = best[b, g : g + 1]
            new = old
            for top, keep in zip(tops, keeps[b]):
                new = jnp.maximum(new, top + (keep - 1.0) * (-NEGATIVE))
            weights = jnp.concatenate(
                [
                    jnp.exp2(half - jnp.maximum(new, top)).astype(BF16)
                    for half, top in zip(halves, tops)
                ],
                axis=0,
            )
            fade = jnp.exp2(old - new)
            best[b, g : g + 1] = new
            vals = [
                jnp.concatenate([v_all[source, i, lanes, :], ones], axis=0) * keep.astype(BF16)
                for source, keep in zip(sources, keeps[b])
            ]
            vals = jnp.concatenate(vals, axis=1)
            pair = 2 * head_dim
            for n in range(per_group // 2):
                cols = slice(2 * n * BLOCK, (2 * n + 2) * BLOCK)
                rows_in = jnp.concatenate([vals[n * pair : (n + 1) * pair], vals[GROUP:]], axis=0)
                out = jnp.dot(rows_in, weights[:, cols], preferred_element_type=F32)
                total[b, g : g + 1, cols] = (
                    total[b, g : g + 1, cols] * fade[:, cols] + out[pair : pair + 1]
                )
                for j in range(2):
                    at = g * GROUP + (2 * n + j) * head_dim
                    side = slice(j * BLOCK, (j + 1) * BLOCK)
                    accum[b, at : at + head_dim] = (
                        accum[b, at : at + head_dim] * fade[:, cols][:, side]
                        + out[j * head_dim : (j + 1) * head_dim, side]
                    )

        units = [(b, g) for b in range(blocks) for g in range(groups)]
        ready = scores_of(*units[0])
        for at, unit in enumerate(units):
            later = scores_of(*units[at + 1]) if at + 1 < len(units) else None
            finish(*unit, ready)
            ready = later

    loads[2].wait()
    remote(k_ref, k_all.at[mate], mate_send.at[0], mate_recv.at[0], mate_id).wait_recv()
    remote(
        v_all.at[mate], v_all.at[mate], mate_send.at[1], mate_recv.at[1], mate_id
    ).wait_recv()
    lax.fori_loop(0, blocks, lambda i, c: (attend(me, mate, i), c)[1], 0)

    for step in range(1, rows):
        origin = row_source(step) * 2
        near, far = origin + core, origin + 1 - core

        def arriving(i, carry, step=step, near=near, far=far):
            place = pl.ds(pl.multiple_of(i * BLOCK, BLOCK), BLOCK)
            remote(
                k_ref.at[place], k_all.at[near, place],
                row_send.at[step - 1, 0, i], row_recv.at[step - 1, 0, i], mate_id,
            ).wait_recv()
            remote(
                k_all.at[near, place], k_all.at[near, place],
                pass_send.at[step - 1, 0, i], pass_recv.at[step - 1, 0, i], mate_id,
            ).start()
            remote(
                v_all.at[near, i], v_all.at[near, i],
                row_send.at[step - 1, 1, i], row_recv.at[step - 1, 1, i], mate_id,
            ).wait_recv()
            remote(
                v_all.at[near, i], v_all.at[near, i],
                pass_send.at[step - 1, 1, i], pass_recv.at[step - 1, 1, i], mate_id,
            ).start()
            remote(
                k_all.at[far, place], k_all.at[far, place],
                pass_send.at[step - 1, 0, i], pass_recv.at[step - 1, 0, i], mate_id,
            ).wait_recv()
            remote(
                v_all.at[far, i], v_all.at[far, i],
                pass_send.at[step - 1, 1, i], pass_recv.at[step - 1, 1, i], mate_id,
            ).wait_recv()
            attend(near, far, i)
            return carry

        lax.fori_loop(0, blocks, arriving, 0)

    for b in range(blocks):
        for g in range(groups):
            parts = []
            share = 1.0 / total[b, g : g + 1]
            for j in range(per_group):
                at = g * GROUP + j * head_dim
                cols = slice(j * BLOCK, (j + 1) * BLOCK)
                parts.append(accum[b, at : at + head_dim] * share[:, cols])
            mixed_ref[b * BLOCK : (b + 1) * BLOCK, g * GROUP : (g + 1) * GROUP] = (
                jnp.concatenate(parts, axis=0).T.astype(BF16)
            )

    key_mate.wait_send()
    value_mate.wait_send()
    for step in range(1, rows):
        near = row_source(step) * 2 + core
        for i in range(blocks):
            place = slice(i * BLOCK, (i + 1) * BLOCK)
            key_row_copy(step, i).wait_send()
            value_row_copy(step, i).wait_send()
            remote(
                k_all.at[near, place], k_all.at[near, place],
                pass_send.at[step - 1, 0, i], pass_recv.at[step - 1, 0, i], mate_id,
            ).wait_send()
            remote(
                v_all.at[near, i], v_all.at[near, i],
                pass_send.at[step - 1, 1, i], pass_recv.at[step - 1, 1, i], mate_id,
            ).wait_send()


def contrast_part(
    n_seq, n_plane, n_event, early, mixed_ref, weight_ref, served_ref, rows_ref, slot_ref, live_ref,
    grad_ref, loss_ref,
    outgoing, contenders, direction, inverse, units, turned, logits, slopes, embed_grads,
    part_out, part_in, event_all, plane_stat, event_stat,
    go_send, go_recv, part_send, part_recv,
    event_send, event_recv, whole_send, whole_recv,
    pstat_send, pstat_recv, estat_send, estat_recv,
):
    points, width = mixed_ref.shape
    capacity = served_ref.shape[1]
    anchors_dev = rows_ref.shape[1]
    chunk = part_out.shape[2]
    cands = n_plane * capacity
    my_event, me, target, source, event_at, steps = early

    def push(src, dst, send, recv, step):
        peer, device = target(step)
        return remote(src, dst.at[me], send.at[peer], recv.at[me], device)

    def pull(dst, send, recv, step):
        peer = source(step)
        return remote(dst.at[peer], dst.at[peer], send.at[peer], recv.at[peer], target(step)[1])

    point_index = lax.broadcasted_iota(jnp.int32, (points, capacity), 0)

    def gather(peer):
        pick = jnp.where(served_ref[pl.ds(peer, 1), :] == point_index, 1.0, 0.0).astype(BF16)
        return jnp.dot(pick.T, mixed_ref[...], preferred_element_type=F32).astype(BF16)

    for step in steps:
        peer = target(step)[0]
        outgoing[peer] = gather(peer)
        push(outgoing.at[peer], contenders, go_send, go_recv, step).start()
    contenders[me] = gather(me)

    anchor_pick = jnp.where(
        rows_ref[...] == lax.broadcasted_iota(jnp.int32, (points, anchors_dev), 0), 1.0, 0.0
    ).astype(BF16)
    anchor_mixed = jnp.dot(anchor_pick.T, mixed_ref[...], preferred_element_type=F32).astype(BF16)

    def project(rows_mixed, at):
        place = slice(at, at + rows_mixed.shape[0])
        embed = jnp.dot(rows_mixed, weight_ref[...], preferred_element_type=F32)
        scale = lax.rsqrt(jnp.sum(embed * embed, axis=-1, keepdims=True) + 1e-06)
        embed = embed * scale
        inverse[place] = scale
        direction[place] = embed
        units[place] = embed.astype(BF16)
        turned[:, place] = rows_mixed.T

    project(anchor_mixed, cands)
    anchors = units[cands:]
    anchors_turned = anchors.T
    live = live_ref[...].astype(F32)
    slots = slot_ref[...]
    slot_index = lax.broadcasted_iota(jnp.int32, (capacity, anchors_dev), 0)

    def correct(peer):
        return jnp.where(slots - peer * capacity == slot_index, 1.0, 0.0)

    sums = jnp.zeros((1, anchors_dev), F32)
    goal = jnp.zeros((1, anchors_dev), F32)
    arrivals = [None] + steps[-1:] + steps[:-1]
    origins = [source(step) if step else me for step in arrivals]
    for at, step in enumerate(arrivals):
        peer = origins[at]
        if step:
            pull(contenders, go_send, go_recv, step).wait_recv()
        place = slice(at * capacity, (at + 1) * capacity)
        project(contenders[peer], at * capacity)
        scores = jnp.dot(units[place], anchors_turned, preferred_element_type=F32)
        scores = scores * (1.0 / SHARPNESS_SCALE)
        grown = jnp.exp(scores)
        logits[place] = grown
        sums = sums + jnp.sum(grown, axis=0, keepdims=True)
        goal = goal + jnp.sum(scores * correct(peer), axis=0, keepdims=True)
    loss_part = jnp.sum(live * (jnp.log(sums) - goal), axis=1, keepdims=True)
    live_part = jnp.sum(live, axis=1, keepdims=True)
    row_index = lax.broadcasted_iota(jnp.int32, (8, 128), 0)
    plane_stat[me] = jnp.where(row_index == 0, loss_part, live_part)
    for step in steps:
        push(plane_stat.at[me], plane_stat, pstat_send, pstat_recv, step).start()

    pull_up = live * (1.0 / SHARPNESS_SCALE)
    share = pull_up / sums
    for at, peer in enumerate(origins):
        place = slice(at * capacity, (at + 1) * capacity)
        slopes[place] = (logits[place] * share - correct(peer) * pull_up).astype(BF16)

    def pull_back(grads, place):
        along = direction[place]
        inner = jnp.sum(along * grads, axis=-1, keepdims=True)
        embed_grads[place] = (inverse[place] * (grads - along * inner)).astype(BF16)

    for at in range(0, cands, anchors_dev):
        place = slice(at, at + anchors_dev)
        pull_back(jnp.dot(slopes[place], anchors, preferred_element_type=F32), place)
    pull_back(
        jnp.dot(slopes[...].T, units[:cands], preferred_element_type=F32),
        slice(cands, cands + anchors_dev),
    )
    parts = [slice(at, at + GROUP) for at in range(0, width, GROUP)]
    for n, cols in enumerate(parts):
        part = jnp.dot(turned[...], embed_grads[:, cols], preferred_element_type=F32)
        part_out[n] = part.astype(BF16).reshape(n_plane, chunk, GROUP)
        for step in steps:
            peer = target(step)[0]
            push(
                part_out.at[n, peer], part_in.at[n], part_send.at[n], part_recv.at[n], step
            ).start()
        part_in[n, me] = part_out[n, me]

    for step in steps:
        pull(plane_stat, pstat_send, pstat_recv, step).wait_recv()
    stat = plane_stat[0]
    for p in range(1, n_plane):
        stat = stat + plane_stat[p]
    event_stat[my_event] = stat

    def event_swap(array, send, recv, step, slot):
        event = event_at(step)
        return remote(
            array.at[my_event], array.at[slot], send.at[event], recv.at[slot], {"event": event}
        )

    for step in range(1, n_event):
        event_swap(event_stat, estat_send, estat_recv, step, my_event).start()

    for n in range(len(parts)):
        for step in steps:
            pull(part_in.at[n], part_send.at[n], part_recv.at[n], step).wait_recv()
        reduced = part_in[n, 0].astype(F32)
        for p in range(1, n_plane):
            reduced = reduced + part_in[n, p].astype(F32)
        event_all[n, my_event] = reduced.astype(BF16)
        for step in range(1, n_event):
            event_swap(
                event_all.at[n], event_send.at[n], event_recv.at[n], step, my_event
            ).start()

    mate_step = (0, 0, 1)
    same_core = [step for step in steps if step[2] == 0]

    def hand_over(n, cols, step):
        block = source(step)
        ref = grad_ref.at[block, :, cols]
        slot = target((step[0], step[1], 1))[0]
        return remote(
            ref, ref, whole_send.at[n, slot], whole_recv.at[n, block], target(mate_step)[1]
        )

    def spread(n, cols, step):
        peer, device = target(step)
        mine = grad_ref.at[me, :, cols]
        return remote(mine, mine, whole_send.at[n, peer], whole_recv.at[n, me], device)

    def landed(n, cols, step):
        peer = source(step)
        theirs = grad_ref.at[peer, :, cols]
        return remote(
            theirs, theirs, whole_send.at[n, peer], whole_recv.at[n, peer], target(step)[1]
        )

    for n, cols in enumerate(parts):
        for step in range(1, n_event):
            event_swap(
                event_all.at[n], event_send.at[n], event_recv.at[n], step, event_at(step)
            ).wait_recv()
        reduced = event_all[n, 0].astype(F32)
        for e in range(1, n_event):
            reduced = reduced + event_all[n, e].astype(F32)
        grad_ref[me, :, cols] = reduced.astype(BF16)
        for step in same_core + [mate_step]:
            spread(n, cols, step).start()

    for n, cols in enumerate(parts):
        for step in same_core:
            landed(n, cols, step).wait_recv()
            hand_over(n, cols, step).start()

    for step in range(1, n_event):
        event_swap(event_stat, estat_send, estat_recv, step, event_at(step)).wait_recv()
    stat = event_stat[0]
    for e in range(1, n_event):
        stat = stat + event_stat[e]
    loss_ref[0, 0] = jnp.max(stat[0:1] / stat[1:2])

    for step in steps:
        peer = target(step)[0]
        push(outgoing.at[peer], contenders, go_send, go_recv, step).wait_send()
        push(plane_stat.at[me], plane_stat, pstat_send, pstat_recv, step).wait_send()
        for n, cols in enumerate(parts):
            push(
                part_out.at[n, peer], part_in.at[n], part_send.at[n], part_recv.at[n], step
            ).wait_send()
    for step in range(1, n_event):
        event_swap(event_stat, estat_send, estat_recv, step, my_event).wait_send()
        for n in range(len(parts)):
            event_swap(
                event_all.at[n], event_send.at[n], event_recv.at[n], step, my_event
            ).wait_send()
    for n, cols in enumerate(parts):
        for step in steps:
            if step[2]:
                landed(n, cols, step).wait_recv()
    for n, cols in enumerate(parts):
        for step in same_core + [mate_step]:
            spread(n, cols, step).wait_send()
        for step in same_core:
            hand_over(n, cols, step).wait_send()


def whole_kernel(
    n_seq, n_plane, n_event, head_dim, n_attend,
    pattern, q_ref, k_ref, v_ref, weight_hbm, served_hbm, rows_hbm, slot_hbm, live_hbm,
    mixed_ref, grad_ref, loss_ref,
    weight_ref, served_ref, rows_ref, slot_ref, live_ref, input_sem, *scratch,
):
    early = seats(n_seq, n_plane, n_event)
    my_event, me, target, source, event_at, steps = early
    pairs = (
        (weight_hbm, weight_ref), (served_hbm, served_ref), (rows_hbm, rows_ref),
        (slot_hbm, slot_ref), (live_hbm, live_ref),
    )
    inputs = [
        pltpu.make_async_copy(src, dst, input_sem.at[n]) for n, (src, dst) in enumerate(pairs)
    ]

    def arrive():
        for load in inputs:
            load.start()
        greet(
            [target(step)[1] for step in steps]
            + [{"event": event_at(step)} for step in range(1, n_event)]
        )

    attend_part(
        n_seq, head_dim, arrive, pattern, q_ref, k_ref, v_ref, mixed_ref, *scratch[:n_attend]
    )
    for load in inputs:
        load.wait()
    contrast_part(
        n_seq, n_plane, n_event, early, mixed_ref, weight_ref, served_ref, rows_ref, slot_ref,
        live_ref, grad_ref, loss_ref, *scratch[n_attend:],
    )


def per_device(
    query, key, value, pattern, out_weight, served, anchor_rows, positive_slot, anchor_live
):
    n_view, n_seq, n_event = (lax.axis_size(name) for name in ("view", "seq", "event"))
    n_plane = n_view * n_seq
    points, width = query.shape[2:]
    senders, capacity = served.shape[2:]
    anchors_dev = anchor_rows.shape[2]
    head_dim = width // HEADS
    blocks = points // BLOCK
    groups = width // GROUP
    wide = GROUP // head_dim * BLOCK
    hops = max(n_seq // 2 - 1, 1)
    chunk = width // n_plane
    cands = senders * capacity
    every = cands + anchors_dev
    parts = width // GROUP
    dma = pltpu.SemaphoreType.DMA

    def sems(*dims):
        return [dma(dims)] * 2

    inputs = [
        pltpu.VMEM((width, width), BF16),
        pltpu.VMEM((senders, capacity), jnp.int32),
        pltpu.VMEM((1, anchors_dev), jnp.int32),
        pltpu.VMEM((1, anchors_dev), jnp.int32),
        pltpu.VMEM((1, anchors_dev), jnp.int32),
        dma((5,)),
    ]
    attend = [
        pltpu.VMEM((points, width), BF16),
        pltpu.VMEM((points, width), BF16),
        pltpu.VMEM((n_seq, points, width), BF16),
        pltpu.VMEM((n_seq, blocks, width, BLOCK), BF16),
        pltpu.VMEM((blocks, groups, 2 * GROUP, wide), BF16),
        pltpu.VMEM((blocks, groups, wide), F32),
        pltpu.VMEM((blocks, groups, wide), F32),
        pltpu.VMEM((blocks, width, BLOCK), F32),
        dma((3,)),
        *sems(2),
        *sems(hops, 2, blocks),
        *sems(hops, 2, blocks),
    ]
    contrast = [
        pltpu.VMEM((senders, capacity, width), BF16),
        pltpu.VMEM((senders, capacity, width), BF16),
        pltpu.VMEM((every, width), F32),
        pltpu.VMEM((every, 1), F32),
        pltpu.VMEM((every, width), BF16),
        pltpu.VMEM((width, every), BF16),
        pltpu.VMEM((cands, anchors_dev), F32),
        pltpu.VMEM((cands, anchors_dev), BF16),
        pltpu.VMEM((every, width), BF16),
        pltpu.VMEM((parts, n_plane, chunk, GROUP), BF16),
        pltpu.VMEM((parts, n_plane, chunk, GROUP), BF16),
        pltpu.VMEM((parts, n_event, chunk, GROUP), BF16),
        pltpu.VMEM((n_plane, 8, 128), F32),
        pltpu.VMEM((n_event, 8, 128), F32),
        *sems(n_plane),
        *sems(parts, n_plane),
        *sems(parts, n_event),
        *sems(parts, n_plane),
        *sems(n_plane),
        *sems(n_event),
    ]
    smem = pl.BlockSpec(memory_space=pltpu.SMEM)
    vmem = pl.BlockSpec(memory_space=pltpu.VMEM)
    mixed, grad, loss = pl.pallas_call(
        functools.partial(whole_kernel, n_seq, n_plane, n_event, head_dim, len(attend)),
        out_shape=(
            jax.ShapeDtypeStruct((points, width), BF16),
            jax.ShapeDtypeStruct((n_plane, chunk, width), BF16),
            jax.ShapeDtypeStruct((1, 1), F32),
        ),
        in_specs=[smem] + [pl.BlockSpec(memory_space=pltpu.HBM)] * 8,
        out_specs=(vmem, vmem, smem),
        scratch_shapes=inputs + attend + contrast,
        compiler_params=pltpu.CompilerParams(
            collective_id=0, has_side_effects=True, vmem_limit_bytes=63 * 1024 * 1024
        ),
    )(
        pattern[0].transpose(1, 0, 2), query[0, 0], key[0, 0], value[0, 0], out_weight,
        served[0, 0], anchor_rows[0], positive_slot[0], anchor_live[0],
    )
    grad = grad.reshape(out_weight.shape).astype(F32)
    return (mixed[None, None], grad, loss[0, 0])


def solution(mesh):
    placed = (
        P("event", "view", "seq", None),
        P("event", "view", "seq", None),
        P("event", "view", "seq", None),
        P("event", "view", "seq", None),
        P(),
        P("event", "view", "seq", None),
        P("event", "view", "seq"),
        P("event", "view", "seq"),
        P("event", "view", "seq"),
    )
    return jax.shard_map(
        per_device,
        mesh=mesh,
        in_specs=placed,
        out_specs=(P("event", "view", "seq", None), P(), P()),
        check_vma=False,
    )
```
